32 devices in a mesh: tm: 4 (over y, core), height: 8 (over z, x).
Axes of the slice: x: 2, y: 2, z: 4, core: 2. Of those that a mesh axis runs over, the one named last changes fastest.
Arguments:
- clip: bfloat16 [16, 8, 128, 256], P('tm', 'height'), may hold values from -6 to 6
- conv_weight: bfloat16 [3, 3, 3, 256, 256], replicated, may hold values from -0.078125 to 0.078125
- down_weight: bfloat16 [3, 256, 256], replicated, may hold values from -0.21875 to 0.21875
- grad_out: bfloat16 [8, 8, 128, 256], P('tm', 'height'), may hold values from -6 to 6
Outputs:
- grad_input: bfloat16 [16, 8, 128, 256], P('tm', 'height')
- grad_conv: float32 [6912, 256], P('height', 'tm')
- grad_down: float32 [768, 256], P('height', 'tm')
The draws below stay inside these ranges and needn't reach their ends.
All inputs are finite; a program needn't handle non-finite values.
Results may differ from the reference program's by a relative error of at most 0.0051.
Values may be sent and summed in bfloat16 or wider, within the bound.
No kernel may reach another device: no remote copies, remote signals or barrier semaphores. Data moves between devices by JAX's collectives and lax.ppermute only.
A program may use at most 128 MiB of HBM per device.

```python
import jax
import jax.numpy as jnp

C = 256
WIDTH = 128
ROWS = 8
CLIPS = 1
ALL_ROWS = 8
FRAMES = 16
OUT_FRAMES = 8


def levels(rng, extent, split, least, top_value):
    factor_of = 1.0
    for position, parts in split:
        heights = jax.random.uniform(jax.random.fold_in(jax.random.fold_in(rng, 6), position), (parts,), jnp.float32, least / len(split), top_value / len(split))
        factor_of = factor_of * jnp.repeat(jnp.exp(heights), extent[position] // parts).reshape((-1,) + (1,) * (len(extent) - 1 - position))
    return factor_of


def centred(key, dims, scale, reach, shards=(), held_as=jnp.bfloat16):
    gain = levels(key, dims, shards, -0.22, 0.18) if shards else 1.0
    array = jax.random.normal(key, dims, jnp.float32) * scale * gain
    return jnp.minimum(jnp.maximum(array, -reach), reach).astype(held_as)


def setup_inputs(seed: int = 0) -> dict:
    keys = jax.random.split(jax.random.key(seed), 5)
    return {
        "clip": centred(keys[0], (FRAMES, ALL_ROWS, WIDTH, C), 1.0, 6.0, ((0, 4), (1, 8))),
        "conv_weight": centred(keys[1], (3, 3, 3, C, C), (27 * C) ** -0.5, 0.078125),
        "down_weight": centred(keys[2], (3, C, C), (3 * C) ** -0.5, 0.21875),
        "grad_out": centred(keys[3], (OUT_FRAMES, ALL_ROWS, WIDTH, C), 1.0, 6.0, ((0, 4), (1, 8))),
    }


def silu_grad(value):
    sig = jax.nn.sigmoid(value)
    return sig * (1.0 + value * (1.0 - sig))

def spread_back(here, later, down_weight):
    chans = here.shape[-1]
    here_flat = here.reshape(-1, chans)
    later_flat = later.reshape(-1, chans)
    even = jnp.dot(later_flat, down_weight[0].T, preferred_element_type=jnp.float32) + jnp.dot(here_flat, down_weight[2].T, preferred_element_type=jnp.float32)
    odd = jnp.dot(later_flat, down_weight[1].T, preferred_element_type=jnp.float32)
    shape = here.shape
    stacked = jnp.stack([even.reshape(shape), odd.reshape(shape)], axis=1)
    return stacked.reshape((2 * shape[0],) + shape[1:]).astype(jnp.bfloat16)

def one_clip(clip, conv_weight, down_weight, grad_out):
    nframes, nrows, ncols, chans = clip.shape
    cells = nframes * nrows * ncols
    inputs = clip.astype(jnp.float32)
    act = jax.nn.silu(inputs).astype(jnp.bfloat16)
    act_pad = jnp.pad(act, ((2, 0), (1, 1), (1, 1), (0, 0)))
    conv = jnp.zeros((cells, chans), jnp.float32)
    for a in range(3):
        for b in range(3):
            patch = jnp.concatenate([act_pad[a:a + nframes, b:b + nrows, c:c + ncols] for c in range(3)], axis=-1).reshape(cells, 3 * chans)
            conv = conv + jnp.dot(patch, conv_weight[a, b].reshape(3 * chans, chans), preferred_element_type=jnp.float32)
    summed = (inputs + conv.reshape(clip.shape)).astype(jnp.bfloat16)
    later = jnp.concatenate([grad_out[1:], jnp.zeros_like(grad_out[:1])], axis=0)
    grad_sum = spread_back(grad_out, later, down_weight)
    half = grad_out.shape[0]
    sum_pad = jnp.pad(summed, ((2, 0), (0, 0), (0, 0), (0, 0)))
    out_flat = grad_out.reshape(-1, chans)
    down_terms = []
    for k in range(3):
        picked = sum_pad[k:k + 2 * half:2].reshape(-1, chans)
        down_terms.append(jnp.dot(picked.T, out_flat, preferred_element_type=jnp.float32))
    grad_down = jnp.concatenate(down_terms, axis=0)
    grad_pad = jnp.pad(grad_sum, ((0, 2), (1, 1), (1, 1), (0, 0)))
    grad_flat = grad_sum.reshape(cells, chans)
    grad_act = jnp.zeros((cells, chans), jnp.float32)
    conv_terms = []
    for a in range(3):
        for b in range(3):
            patch = jnp.concatenate([act_pad[a:a + nframes, b:b + nrows, c:c + ncols] for c in range(3)], axis=-1).reshape(cells, 3 * chans)
            conv_terms.append(jnp.dot(patch.T, grad_flat, preferred_element_type=jnp.float32))
            back = jnp.concatenate([grad_pad[2 - a:2 - a + nframes, 2 - b:2 - b + nrows, 2 - c:2 - c + ncols] for c in range(3)], axis=-1).reshape(cells, 3 * chans)
            flipped = jnp.transpose(conv_weight[a, b], (0, 2, 1)).reshape(3 * chans, chans)
            grad_act = grad_act + jnp.dot(back, flipped, preferred_element_type=jnp.float32)
    grad_conv = jnp.concatenate(conv_terms, axis=0)
    grad_input = (grad_sum.astype(jnp.float32) + grad_act.reshape(clip.shape) * silu_grad(inputs)).astype(jnp.bfloat16)
    return (grad_input, grad_conv, grad_down)

def reference(clip, conv_weight, down_weight, grad_out):
    inputs_list = []
    grad_conv = jnp.zeros((27 * C, C), jnp.float32)
    grad_down = jnp.zeros((3 * C, C), jnp.float32)
    for index in range(CLIPS):
        lower = index * ROWS
        piece_in, piece_conv, piece_down = one_clip(clip[:, lower:lower + ROWS], conv_weight, down_weight, grad_out[:, lower:lower + ROWS])
        inputs_list.append(piece_in)
        grad_conv = grad_conv + piece_conv
        grad_down = grad_down + piece_down
    return (jnp.concatenate(inputs_list, axis=1), grad_conv, grad_down)
```

```python
import functools

import jax
import jax.numpy as jnp
from jax import lax
from jax.experimental import pallas as pl
from jax.experimental.pallas import tpu as pltpu
from jax.sharding import PartitionSpec as P

F32 = jnp.float32
BF16 = jnp.bfloat16
VMEM_LIMIT = 56 * 1024 * 1024


def dot(left, right):
    return jnp.dot(left, right, preferred_element_type=F32)


def dot_nt(left, right):
    return lax.dot_general(left, right, (((1,), (1,)), ((), ())), preferred_element_type=F32)


def shifted_rows(value, step, period):
    if step == 0:
        return value
    rows = value.shape[0]
    moved = pltpu.roll(value, (-step) % rows, 0)
    place = lax.broadcasted_iota(jnp.int32, value.shape, 0) % period + step
    return jnp.where(jnp.logical_and(place >= 0, place < period), moved, 0.0)


def pack_halves(low, high, core):
    lane = lax.broadcasted_iota(jnp.int32, low.shape, 1)
    width = low.shape[1] // 2
    left = lane < width
    first = jnp.where(left, low, pltpu.roll(high, width, 1))
    second = jnp.where(left, pltpu.roll(low, width, 1), high)
    mine = core == 0
    return jnp.where(mine, second, first), jnp.where(mine, first, second)


def terms_kernel(dims, core_ref, clip_ref, up_ref, up_next_ref, here_ref, next_ref, low_ref, low_next_ref,
                 down_ref, grad_ref, act_ref, back_ref, send_ref, keep_ref, turned, total):
    frames, cols, chans, count = dims
    cells = frames * cols
    half = frames // 2
    core = core_ref[0]
    value = clip_ref[...].astype(F32)
    act = value / (1.0 + jnp.exp(-value))
    act = act.astype(BF16).astype(F32)
    for c in range(3):
        moved = shifted_rows(act, c - 1, cols)
        act_ref[:, c * chans : (c + 1) * chans] = moved.astype(BF16)
        turned[c * chans : (c + 1) * chans, :] = moved.T.astype(BF16)
    pairs = ((low_ref, low_next_ref), (here_ref, next_ref), (up_ref, up_next_ref))
    for b, (own, later) in enumerate(pairs):
        every = jnp.concatenate([own[...], later[...]], axis=0)
        back_ref[b] = every.T
        here = every[: (half + 1) * cols]
        after = every[cols : (half + 2) * cols]
        even = (dot_nt(after, down_ref[0]) + dot_nt(here, down_ref[2])).astype(BF16)
        odd = dot_nt(after, down_ref[1]).astype(BF16)
        for u in range(half + 1):
            grad_ref[b, 2 * u * cols : (2 * u + 1) * cols] = even[u * cols : (u + 1) * cols]
            grad_ref[b, (2 * u + 1) * cols : (2 * u + 2) * cols] = odd[u * cols : (u + 1) * cols]
    wide = 3 * chans
    lanes = chans // 2
    for a in range(3):
        for b in range(3):
            begin = (2 - a) * cols
            part = dot(turned[...], grad_ref[b, begin : begin + cells])
            row = (a * 3 + b) * wide
            for y in range(2):
                total[y, row : row + wide] = part[:, y * lanes : (y + 1) * lanes]
    block = 9 * wide // count
    for h in range(count):
        for y in range(2):
            low = total[y, h * block : h * block + block // 2]
            high = total[y, h * block + block // 2 : (h + 1) * block]
            send, keep = pack_halves(low, high, core)
            send_ref[y, h] = send.astype(BF16)
            keep_ref[y, h] = keep.astype(BF16)


def down_kernel(dims, core_ref, clip_ref, act_ref, back_ref, weight_ref, send_ref, keep_ref, cross, total):
    frames, cols, chans, count = dims
    half = frames // 2
    core = core_ref[0]
    wide = 3 * chans

    def pick(value, parity):
        return jnp.concatenate([value[(2 * u + parity) * cols : (2 * u + parity + 1) * cols] for u in range(half)], axis=0)

    sides = (pick(act_ref[...], 0), pick(act_ref[...], 1))
    clips = (pick(clip_ref[...], 0), pick(clip_ref[...], 1))
    for s in range(5):
        begin = ((4 - s + s % 2) // 2) * cols
        for b in range(3):
            cross[s, b] = dot(back_ref[b, :, begin : begin + half * cols], sides[s % 2]).astype(BF16)
    lanes = chans // 2
    for k in range(3):
        begin = ((2 - k + k % 2) // 2) * cols
        part = dot(back_ref[1, :, begin : begin + half * cols], clips[k % 2])
        for a in range(3):
            for b in range(3):
                part = part + dot(cross[a + k, b], weight_ref[a * 3 + b])
        flipped = part.T
        for y in range(2):
            total[y, k * chans : (k + 1) * chans] = flipped[:, y * lanes : (y + 1) * lanes]
    block = 3 * chans // count
    for h in range(count):
        for y in range(2):
            low = total[y, h * block : h * block + block // 2]
            high = total[y, h * block + block // 2 : (h + 1) * block]
            send, keep = pack_halves(low, high, core)
            send_ref[y, h] = send.astype(BF16)
            keep_ref[y, h] = keep.astype(BF16)


def input_kernel(dims, clip_ref, grad_ref, weight_ref, out_ref):
    frames, cols, chans, _ = dims
    cells = frames * cols
    acc = [jnp.zeros((cells, chans), F32) for _ in range(3)]
    for a in range(3):
        for b in range(3):
            begin = (2 - a) * cols
            grads = grad_ref[b, begin : begin + cells]
            for c in range(3):
                acc[c] = acc[c] + dot_nt(grads, weight_ref[a * 3 + b, c * chans : (c + 1) * chans])
    grad_act = acc[1]
    for c in (0, 2):
        grad_act = grad_act + shifted_rows(acc[c], 1 - c, cols)
    value = clip_ref[...].astype(F32)
    sig = 1.0 / (1.0 + jnp.exp(-value))
    own = grad_ref[1, :cells].astype(F32)
    out_ref[...] = (own + grad_act * (sig * (1.0 + value * (1.0 - sig)))).astype(BF16)


def vmem():
    return pl.BlockSpec(memory_space=pltpu.VMEM)


def smem():
    return pl.BlockSpec(memory_space=pltpu.SMEM)


def shape(dims, dtype):
    return jax.ShapeDtypeStruct(dims, dtype)


def call(kernel, scalars, args, outs, scratch=(), flops=0):
    size = sum(a.size * a.dtype.itemsize for a in args)
    return pl.pallas_call(
        kernel,
        out_shape=outs,
        in_specs=[smem()] * len(scalars) + [vmem()] * len(args),
        out_specs=jax.tree.map(lambda _: vmem(), outs),
        scratch_shapes=list(scratch),
        compiler_params=pltpu.CompilerParams(vmem_limit_bytes=VMEM_LIMIT),
        cost_estimate=pl.CostEstimate(flops=flops, bytes_accessed=size, transcendentals=0),
    )(*scalars, *args)


def halved(ref, axis, index):
    lead = ref.shape[:-2]
    rest = lead[:axis] + lead[axis + 1 :]
    for flat in range(functools.reduce(lambda p, q: p * q, rest, 1)):
        spot, left = [], flat
        for extent in reversed(rest):
            spot.insert(0, left % extent)
            left //= extent
        yield tuple(spot), tuple(spot[:axis]) + (index,) + tuple(spot[axis:])


def first_kernel(axes, cuts, bits_ref, conv_keep, conv_got, down_keep, down_got, *outs):
    rows = conv_keep.shape[-2]

    def summed(where, begin, end):
        parts = []
        if begin < rows:
            top = min(end, rows)
            parts.append(conv_keep[where + (slice(begin, top),)].astype(F32) + conv_got[where + (slice(begin, top),)].astype(F32))
        if end > rows:
            parts.append(down_keep[where].astype(F32) + down_got[where].astype(F32))
        return parts[0] if len(parts) == 1 else jnp.concatenate(parts, axis=0)

    for g, axis in enumerate(axes):
        mine = bits_ref[g]
        send, keep = outs[2 * g], outs[2 * g + 1]
        for to, where in halved(conv_keep, axis, 1 - mine):
            send[to] = summed(where, *cuts[g]).astype(BF16)
        for to, where in halved(conv_keep, axis, mine):
            keep[to] = summed(where, *cuts[g])


def fold_kernel(axes, bits_ref, *refs):
    count = len(axes)
    for g, axis in enumerate(axes):
        mine = bits_ref[g]
        held, got = refs[2 * g], refs[2 * g + 1]
        send, keep = refs[2 * count + 2 * g], refs[2 * count + 2 * g + 1]
        for to, where in halved(held, axis, 1 - mine):
            send[to] = (held[where] + got[where].astype(F32)).astype(BF16)
        for to, where in halved(held, axis, mine):
            keep[to] = held[where] + got[where].astype(F32)


def join_kernel(rows, *refs):
    groups = (len(refs) - 2) // 2
    conv_ref, down_ref = refs[-2:]
    parts = []
    for g in range(groups):
        parts.append(refs[2 * g][...] + refs[2 * g + 1][...].astype(F32))
    every = jnp.concatenate(parts, axis=0)
    width = every.shape[1] // 2
    for ref, begin, end in ((conv_ref, 0, rows), (down_ref, rows, every.shape[0])):
        piece = every[begin:end]
        ref[: end - begin] = piece[:, :width]
        ref[end - begin :] = pltpu.roll(piece, width, 1)[:, :width]


def swapped(value, axis, bit):
    count = lax.axis_size(axis)
    return lax.ppermute(value, axis, [(i, i ^ (1 << bit)) for i in range(count)])


def scattered(conv, down, tm_index, height_index):
    count = lax.axis_size("height")
    nbits = count.bit_length() - 1
    got = [swapped(send, "tm", 0) for send, _ in (conv, down)]
    rows = conv[0].shape[-2]
    total = rows + down[0].shape[-2]
    lead = (2,) * (1 + nbits)
    lanes = conv[0].shape[-1]

    def split(value):
        return value.reshape(lead + value.shape[-2:])

    links = [("tm", 1)] + [("height", i) for i in range(nbits)]
    position = {link: (0 if link[0] == "tm" else nbits - link[1]) for link in links}
    tops = links[:3]
    rest = links[3:]
    orders = [tops[g:] + tops[:g] + rest for g in range(3)]
    third = total // 3
    cuts = [(g * third, (g + 1) * third) for g in range(3)]

    def bit_of(link):
        index = tm_index if link[0] == "tm" else height_index
        return lax.shift_right_logical(index, link[1]) & 1

    left = [list(links) for _ in range(3)]

    def axis_of(g, link):
        ahead = [l for l in left[g] if position[l] < position[link]]
        return len(ahead)

    held = None
    for step in range(len(links)):
        now = [orders[g][step] for g in range(3)]
        axes = [axis_of(g, now[g]) for g in range(3)]
        bits = jnp.stack([bit_of(link) for link in now]).astype(jnp.int32)
        depth = len(links) - step - 1
        outs = []
        for g in range(3):
            dims = (2,) * depth + (third, lanes)
            outs += [shape(dims, BF16), shape(dims, F32)]
        if step == 0:
            args = [split(conv[1]), split(got[0]), split(down[1]), split(got[1])]
            kernel = functools.partial(first_kernel, axes, cuts)
        else:
            args = held
            kernel = functools.partial(fold_kernel, axes)
        result = call(kernel, [bits], args, outs)
        held = []
        for g in range(3):
            arrived = swapped(result[2 * g], *now[g])
            held += [result[2 * g + 1], arrived]
            left[g].remove(now[g])
    return call(
        functools.partial(join_kernel, rows), [], held,
        (shape((2 * rows, lanes // 2), F32), shape((2 * (total - rows), lanes // 2), F32)),
    )


def body(clip, conv_weight, down_weight, grad_out):
    nframes, nrows, ncols, chans = clip.shape
    half = grad_out.shape[0]
    cells = nframes * ncols
    outs = half * ncols
    tm_count, count = lax.axis_size("tm"), lax.axis_size("height")
    tm_index, height_index = lax.axis_index("tm"), lax.axis_index("height")
    mine = grad_out.reshape(outs, chans)

    def moved(rows, frames):
        pairs = []
        for t in range(tm_count):
            for h in range(count):
                to_t, to_h = t - frames, h + rows
                if 0 <= to_t < tm_count and 0 <= to_h < count:
                    pairs.append((t * count + h, to_t * count + to_h))
        return lax.ppermute(mine, ("tm", "height"), pairs)

    later = moved(0, 1)
    above, below = moved(1, 0), moved(-1, 0)
    above_later, below_later = moved(1, 1), moved(-1, 1)
    flat = clip.reshape(cells, chans)
    weight = conv_weight.reshape(9, 3 * chans, chans)
    core = (tm_index & 1).reshape(1).astype(jnp.int32)
    dims = (nframes, ncols, chans, count)
    wide = 3 * chans
    lanes = chans // 2
    grads, act, back, conv_send, conv_keep = call(
        functools.partial(terms_kernel, dims), [core],
        [flat, above, above_later, mine, later, below, below_later, down_weight],
        (
            shape((3, cells + 2 * ncols, chans), BF16),
            shape((cells, wide), BF16),
            shape((3, chans, 2 * outs), BF16),
            shape((2, count, 9 * wide // count // 2, lanes), BF16),
            shape((2, count, 9 * wide // count // 2, lanes), BF16),
        ),
        [pltpu.VMEM((wide, cells), BF16), pltpu.VMEM((2, 9 * wide, lanes), F32)],
        flops=2 * 9 * wide * cells * chans,
    )
    down_send, down_keep = call(
        functools.partial(down_kernel, dims), [core],
        [flat, act, back, weight],
        (
            shape((2, count, wide // count // 2, lanes), BF16),
            shape((2, count, wide // count // 2, lanes), BF16),
        ),
        [pltpu.VMEM((5, 3, chans, wide), BF16), pltpu.VMEM((2, wide, lanes), F32)],
        flops=4 * 9 * wide * cells * chans,
    )
    grad_conv, grad_down = scattered((conv_send, conv_keep), (down_send, down_keep), tm_index, height_index)
    grad_input = call(
        functools.partial(input_kernel, dims), [], [flat, grads, weight],
        shape((cells, chans), BF16),
        flops=2 * 9 * wide * cells * chans,
    )
    return (grad_input.reshape(clip.shape), grad_conv, grad_down)


def solution(mesh):
    placed = (P("tm", "height", None, None), P(), P(), P("tm", "height", None, None))
    return jax.shard_map(
        body,
        mesh=mesh,
        in_specs=placed,
        out_specs=(P("tm", "height", None, None), P("height", "tm"), P("height", "tm")),
        check_vma=False,
    )
```

```python
import functools
import math

import jax
import jax.numpy as jnp
from jax import lax
from jax.experimental import pallas as pl
from jax.experimental.pallas import tpu as pltpu
from jax.sharding import PartitionSpec as P

F32 = jnp.float32
BF16 = jnp.bfloat16
MIB = 1024 * 1024


def dot(left, right):
    return jnp.dot(left, right, preferred_element_type=F32)


def dot_nt(left, right):
    return lax.dot_general(left, right, (((1,), (1,)), ((), ())), preferred_element_type=F32)


def shifted_rows(value, step, period):
    if step == 0:
        return value
    rows = value.shape[0]
    moved = pltpu.roll(value, (-step) % rows, 0)
    place = lax.broadcasted_iota(jnp.int32, value.shape, 0) % period + step
    return jnp.where(jnp.logical_and(place >= 0, place < period), moved, 0.0)


def channel_of(place, group, core):
    return (place // group * 2 + core) * group + place % group


def picker(chans, group, core):
    dims = (chans, chans // 2)
    wanted = channel_of(lax.broadcasted_iota(jnp.int32, dims, 1), group, core)
    return (lax.broadcasted_iota(jnp.int32, dims, 0) == wanted).astype(F32).astype(BF16)


def lay_window(window, core, own, other, first, second, frames):
    window[pl.ds(0, frames)] = first[...] + second[...]
    window[pl.ds(pl.multiple_of(frames * (1 + core), frames), frames)] = own[...]
    window[pl.ds(pl.multiple_of(frames * (2 - core), frames), frames)] = other[...]


def silu(value):
    return value / (1.0 + jnp.exp(-value))


def halved(lead, axis, index):
    rest = lead[:axis] + lead[axis + 1 :]
    for flat in range(math.prod(rest)):
        spot, left = [], flat
        for extent in reversed(rest):
            spot.insert(0, left % extent)
            left //= extent
        yield tuple(spot), tuple(spot[:axis]) + (index,) + tuple(spot[axis:])


def bit_of(spot_ref, link):
    return lax.shift_right_logical(spot_ref[link[0]], link[1]) & 1


def split_into(send, keep, lead, axis, mine, read):
    for to, where in halved(lead, axis, 1 - mine):
        send[to] = read(where).astype(send.dtype)
    for to, where in halved(lead, axis, mine):
        keep[to] = read(where)


def terms_kernel(plan, spot_ref, clip_ref, clip_other, first_ref, second_ref, here_ref, here_other, high_ref, high_other,
                 low_ref, low_other, down_ref, window_ref, even_ref, odd_ref, *rest):
    outs, (clips, even_t, odd_t, cross, spread, total) = rest[:-6], rest[-6:]
    cols, chans, group = plan.cols, plan.chans, plan.group
    core = spot_ref[0] & 1
    rows = clip_ref.shape[0]
    span = here_ref.shape[0]
    for k in range(3):
        spread[k * chans : (k + 1) * chans] = down_ref[k].T
    lay_window(clips, core, clip_ref, clip_other, first_ref, second_ref, rows)
    act = silu(clips[...].astype(F32)).astype(BF16)
    act = dot(act, picker(chans, group, core))
    part = chans // 2
    for c in range(3):
        moved = shifted_rows(act, c - 1, cols).astype(BF16)
        for f in range(3 * rows // cols // 2):
            to = slice(f * cols, (f + 1) * cols)
            lanes = slice(c * part, (c + 1) * part)
            for natural, turned, at in ((even_ref, even_t, 2 * f), (odd_ref, odd_t, 2 * f + 1)):
                piece = moved[at * cols : (at + 1) * cols]
                natural[to, lanes] = piece
                turned[lanes, to] = piece.T
    for b, (own, other) in enumerate(((low_ref, low_other), (here_ref, here_other), (high_ref, high_other))):
        window_ref[b, pl.ds(pl.multiple_of(span * core, span), span)] = own[...]
        window_ref[b, pl.ds(pl.multiple_of(span * (1 - core), span), span)] = other[...]
    for b in range(3):
        for s in range(5):
            turned = (even_t, odd_t)[s % 2]
            cells = turned[:, s // 2 * cols : s // 2 * cols + 2 * span]
            cross[b, :, s * chans : (s + 1) * chans] = dot(cells, window_ref[b]).astype(BF16)
    wide = 3 * part
    for a in range(3):
        for b in range(3):
            value = dot(cross[b, :, a * chans : (a + 3) * chans], spread[...])
            begin = (a * 3 + b) * wide
            while begin < (a * 3 + b + 1) * wide:
                h = begin // plan.rows
                end = min((h + 1) * plan.rows, (a * 3 + b + 1) * wide)
                where = plan.spot(h)
                for y in range(2):
                    total[(y,) + where + (slice(begin - h * plan.rows, end - h * plan.rows),)] = value[
                        begin - (a * 3 + b) * wide : end - (a * 3 + b) * wide, y * part : (y + 1) * part
                    ]
                begin = end
    for g in range(3):
        link = plan.orders[g][0]
        begin, end = plan.cuts[g]
        split_into(
            outs[2 * g], outs[2 * g + 1], plan.lead, plan.axis(g, 0), bit_of(spot_ref, link),
            lambda where: total[where + (slice(begin, end),)],
        )


def down_kernel(plan, spot_ref, clip_ref, clip_other, first_ref, second_ref, window_ref, even_ref, odd_ref, weight_ref,
                send_ref, keep_ref, clips, back, picked, total):
    cols, chans, group = plan.cols, plan.chans, plan.group
    core = spot_ref[0] & 1
    rows = clip_ref.shape[0]
    span = window_ref.shape[1]
    part = chans // 2
    wide = 3 * part
    for b in range(3):
        back[b] = window_ref[b].T
    lay_window(clips, core, clip_ref, clip_other, first_ref, second_ref, rows)
    dims = (chans, chans)
    place = lax.broadcasted_iota(jnp.int32, dims, 1)
    wanted = channel_of(place % part, group, place // part)
    order = (lax.broadcasted_iota(jnp.int32, dims, 0) == wanted).astype(F32).astype(BF16)
    mine = (lax.broadcasted_iota(jnp.int32, (1, chans), 1) // part == core).astype(F32).astype(BF16)
    dims = (part, chans)
    wanted = channel_of(lax.broadcasted_iota(jnp.int32, dims, 0), group, core)
    pick = (lax.broadcasted_iota(jnp.int32, dims, 1) == wanted).astype(F32).astype(BF16)
    for b in range(3):
        for a in range(3):
            for c in range(3):
                block = weight_ref[a * 3 + b, c * chans : (c + 1) * chans]
                block = dot(dot(pick, block).astype(BF16), order).astype(BF16)
                picked[b, a * wide + c * part : a * wide + (c + 1) * part] = block
    clip_list = dot(clips[...], order).astype(BF16) * mine
    halves = []
    for parity in range(2):
        halves.append(jnp.concatenate(
            [clip_list[(2 * f + parity) * cols : (2 * f + parity + 1) * cols] for f in range(3 * rows // cols // 2)], axis=0
        ))
    sums = [None] * 3
    for k in range(3):
        begin = (1 + k // 2) * cols
        sums[k] = dot(back[1], halves[k % 2][begin : begin + span])
    for b in range(3):
        cross = []
        for s in range(5):
            cells = (even_ref, odd_ref)[s % 2][s // 2 * cols : s // 2 * cols + span]
            cross.append(dot(back[b], cells).astype(BF16))
        for k in range(3):
            sums[k] = sums[k] + dot(jnp.concatenate(cross[k : k + 3], axis=1), picked[b])
    for k in range(3):
        flipped = sums[k].T
        for parity in range(2):
            for y in range(2):
                total[parity, y, k * part : (k + 1) * part] = flipped[
                    parity * part : (parity + 1) * part, y * part : (y + 1) * part
                ]
    for h in range(math.prod(plan.lead[1:])):
        for y in range(2):
            where = (y,) + plan.spot(h)
            piece = slice(h * plan.down_rows, (h + 1) * plan.down_rows)
            send_ref[where] = total[1 - core, y, piece].astype(BF16)
            keep_ref[where] = total[core, y, piece]


def down_split_kernel(plan, spot_ref, keep_ref, got_ref, send, keep):
    split_into(
        send, keep, plan.lead, plan.axis(0, 0), bit_of(spot_ref, plan.orders[0][0]),
        lambda where: keep_ref[where] + got_ref[where].astype(F32),
    )


def fold_kernel(plan, step, spot_ref, *refs):
    extra = 2 if step == 1 else 0
    ins, outs = refs[: 6 + extra], refs[6 + extra :]
    for g in range(3):
        link = plan.orders[g][step]
        axis = plan.axis(g, step)
        mine = bit_of(spot_ref, link)
        held, got = ins[2 * g], ins[2 * g + 1]

        def read(where):
            value = held[where] + got[where].astype(F32)
            if step == 1 and g == 0:
                value = jnp.concatenate([value, ins[6][where] + ins[7][where].astype(F32)], axis=0)
            return value

        lead = plan.lead[step:]
        if step < 3:
            split_into(outs[2 * g], outs[2 * g + 1], lead, axis, mine, read)
        else:
            third = held.shape[-2]
            for to, where in halved(lead, axis, 1 - mine):
                outs[0][to + (slice(g * third, (g + 1) * third),)] = read(where).astype(BF16)
            for to, where in halved(lead, axis, mine):
                outs[1][to + (slice(g * third, (g + 1) * third),)] = read(where)


def late_kernel(plan, step, spot_ref, held, got, send, keep):
    link = plan.orders[0][step]
    split_into(
        send, keep, plan.lead[step:], plan.axis(0, step), bit_of(spot_ref, link),
        lambda where: held[where] + got[where].astype(F32),
    )


def last_kernel(held, got, out):
    out[...] = held[...] + got[...].astype(F32)


def join_kernel(plan, spot_ref, mine_ref, other_ref, conv_ref, down_ref, turned, down_turned):
    core = spot_ref[0] & 1
    group = plan.group
    rows, down_rows = plan.rows, plan.down_rows
    own, other = mine_ref[...], other_ref[...]
    first, second = jnp.where(core == 0, own, other), jnp.where(core == 0, other, own)

    def merged(begin, end):
        pieces = []
        for at in range(begin, end, group):
            pieces += [first[at : at + group], second[at : at + group]]
        return pieces

    cut = plan.cuts[0][1]
    conv = merged(0, cut) + merged(cut + down_rows, rows + down_rows)
    down = merged(cut, cut + down_rows)
    width = own.shape[1] // 2
    for ref, pieces, space in ((conv_ref, conv, turned), (down_ref, down, down_turned)):
        space[...] = jnp.concatenate(pieces, axis=0).T
        ref[...] = space[pl.ds(pl.multiple_of(core * width, width), width)]


def input_kernel(plan, spot_ref, clip_ref, window_ref, next_low, next_here, next_high, down_ref, weight_ref, out_ref, grads):
    cols, chans = plan.cols, plan.chans
    cells = clip_ref.shape[0]
    span = next_here.shape[0]
    half = span // cols
    core = spot_ref[0] & 1
    for b, later in enumerate((next_low, next_here, next_high)):
        begin = pl.multiple_of(core * span, span)
        own = window_ref[b, pl.ds(begin, span)]
        following = jnp.where(core == 0, window_ref[b, span:], later[...])
        every = jnp.concatenate([own, following], axis=0)
        here = every[: (half + 1) * cols]
        after = every[cols : (half + 2) * cols]
        even = (dot_nt(after, down_ref[0]) + dot_nt(here, down_ref[2])).astype(BF16)
        odd = dot_nt(after, down_ref[1]).astype(BF16)
        for u in range(half + 1):
            grads[b, 2 * u * cols : (2 * u + 1) * cols] = even[u * cols : (u + 1) * cols]
            grads[b, (2 * u + 1) * cols : (2 * u + 2) * cols] = odd[u * cols : (u + 1) * cols]
    acc = [jnp.zeros((cells, chans), F32) for _ in range(3)]
    for a in range(3):
        for b in range(3):
            begin = (2 - a) * cols
            part = grads[b, begin : begin + cells]
            for c in range(3):
                acc[c] = acc[c] + dot_nt(part, weight_ref[a * 3 + b, c * chans : (c + 1) * chans])
    grad_act = acc[1]
    for c in (0, 2):
        grad_act = grad_act + shifted_rows(acc[c], 1 - c, cols)
    value = clip_ref[...].astype(F32)
    sig = 1.0 / (1.0 + jnp.exp(-value))
    own = grads[1, :cells].astype(F32)
    out_ref[...] = (own + grad_act * (sig * (1.0 + value * (1.0 - sig)))).astype(BF16)


def shape(dims, dtype):
    return jax.ShapeDtypeStruct(dims, dtype)


def call(kernel, scalars, args, outs, scratch=(), flops=0, limit=48):
    vmem, smem = pl.BlockSpec(memory_space=pltpu.VMEM), pl.BlockSpec(memory_space=pltpu.SMEM)
    size = sum(a.size * a.dtype.itemsize for a in args)
    return pl.pallas_call(
        kernel,
        out_shape=outs,
        in_specs=[smem] * len(scalars) + [vmem] * len(args),
        out_specs=jax.tree.map(lambda _: vmem, outs),
        scratch_shapes=list(scratch),
        compiler_params=pltpu.CompilerParams(vmem_limit_bytes=limit * MIB),
        cost_estimate=pl.CostEstimate(flops=flops, bytes_accessed=size, transcendentals=0),
    )(*scalars, *args)


class Plan:
    def __init__(self, count, cols, chans):
        nbits = count.bit_length() - 1
        self.cols, self.chans = cols, chans
        self.rows, self.down_rows = 27 * chans // count // 2, 3 * chans // count // 2
        self.group = math.gcd(16, math.gcd(self.rows, self.down_rows))
        self.lead = (2,) * (1 + nbits)
        links = [(0, 1)] + [(1, i) for i in range(nbits)]
        self.place = {link: (0 if link[0] == 0 else nbits - link[1]) for link in links}
        tops, tail = links[:3], links[3:]
        self.orders = [tops[g:] + tops[:g] + tail for g in range(3)]
        total = self.rows + self.down_rows
        self.third = total // 3
        cut = self.third - self.down_rows
        self.cuts = [(0, cut), (cut, cut + self.third), (cut + self.third, self.rows)]

    def spot(self, h):
        nbits = len(self.lead) - 1
        return tuple(h >> (nbits - 1 - i) & 1 for i in range(nbits))

    def axis(self, g, step):
        order = self.orders[g]
        return sum(self.place[link] < self.place[order[step]] for link in order[step + 1 :])


def swapped(value, link):
    axis = ("tm", "height")[link[0]]
    return lax.ppermute(value, axis, [(i, i ^ (1 << link[1])) for i in range(lax.axis_size(axis))])


def body(clip, conv_weight, down_weight, grad_out):
    nframes, nrows, ncols, chans = clip.shape
    half = grad_out.shape[0]
    cells, span = nframes * ncols, half * ncols
    tm_count, count = lax.axis_size("tm"), lax.axis_size("height")
    plan = Plan(count, ncols, chans)
    spot = jnp.stack([lax.axis_index("tm"), lax.axis_index("height")]).astype(jnp.int32)
    mine = grad_out.reshape(span, chans)
    flat = clip.reshape(cells, chans)
    weight = conv_weight.reshape(9, 3 * chans, chans)
    core_link = (0, 0)

    high = lax.ppermute(mine, "height", [(i, i + 1) for i in range(count - 1)])
    low = lax.ppermute(mine, "height", [(i + 1, i) for i in range(count - 1)])
    first = lax.ppermute(flat, "tm", [(i, i + 1) for i in range(1, tm_count - 1, 2)])
    second = lax.ppermute(flat, "tm", [(i, i + 2) for i in range(1, tm_count - 2, 2)])
    clip_other = swapped(flat, core_link)
    mine_other = swapped(mine, core_link)
    high_other, low_other = swapped(high, core_link), swapped(low, core_link)
    back_pairs = [(i + 1, i) for i in range(1, tm_count - 1, 2)]
    next_here, next_low, next_high = (lax.ppermute(v, "tm", back_pairs) for v in (mine, low, high))

    part = chans // 2
    wide = 3 * part
    lead = plan.lead
    outs = [shape((3, 2 * span, chans), BF16), shape((3 * cells // 2, wide), BF16), shape((3 * cells // 2, wide), BF16)]
    for begin, end in plan.cuts:
        outs += [shape(lead[1:] + (end - begin, part), BF16), shape(lead[1:] + (end - begin, part), F32)]
    result = call(
        functools.partial(terms_kernel, plan), [spot],
        [flat, clip_other, first, second, mine, mine_other, high, high_other, low, low_other, down_weight],
        outs,
        [
            pltpu.VMEM((3 * cells, chans), BF16),
            pltpu.VMEM((wide, 3 * cells // 2), BF16),
            pltpu.VMEM((wide, 3 * cells // 2), BF16),
            pltpu.VMEM((3, wide, 5 * chans), BF16),
            pltpu.VMEM((3 * chans, chans), BF16),
            pltpu.VMEM(lead + (plan.rows, part), F32),
        ],
        flops=2 * 9 * wide * 3 * chans * chans,
    )
    window, even, odd = result[:3]
    held = []
    for g in range(3):
        held += [result[4 + 2 * g], swapped(result[3 + 2 * g], plan.orders[g][0])]

    down_dims = lead + (plan.down_rows, part)
    down_send, down_keep = call(
        functools.partial(down_kernel, plan), [spot],
        [flat, clip_other, first, second, window, even, odd, weight],
        [shape(down_dims, BF16), shape(down_dims, F32)],
        [
            pltpu.VMEM((3 * cells, chans), BF16),
            pltpu.VMEM((3, chans, 2 * span), BF16),
            pltpu.VMEM((3, 3 * wide, chans), BF16),
            pltpu.VMEM((2, 2, wide, part), F32),
        ],
        flops=2 * 9 * wide * 3 * chans * chans,
    )
    send, keep = call(
        functools.partial(down_split_kernel, plan), [spot], [down_keep, swapped(down_send, core_link)],
        [shape(down_dims[1:], BF16), shape(down_dims[1:], F32)], limit=8,
    )
    held += [keep, swapped(send, plan.orders[0][0])]
    grad_input = call(
        functools.partial(input_kernel, plan), [spot],
        [flat, window, next_low, next_here, next_high, down_weight, weight],
        shape((cells, chans), BF16),
        [pltpu.VMEM((3, (2 * half + 2) * ncols, chans), BF16)],
        flops=2 * 27 * chans * cells * chans,
    )
    for step in (1, 2):
        dims = lead[step + 1 :] + (plan.third, part)
        result = call(
            functools.partial(fold_kernel, plan, step), [spot], held,
            [shape(dims, BF16), shape(dims, F32)] * 3, limit=16,
        )
        held = []
        for g in range(3):
            held += [result[2 * g + 1], swapped(result[2 * g], plan.orders[g][step])]
    for step in range(3, len(lead)):
        dims = lead[step + 1 :] + (3 * plan.third, part)
        kernel = fold_kernel if step == 3 else late_kernel
        send, keep = call(
            functools.partial(kernel, plan, step), [spot], held, [shape(dims, BF16), shape(dims, F32)], limit=8
        )
        held = [keep, swapped(send, plan.orders[0][step])]
    total = call(last_kernel, [], held, shape((3 * plan.third, part), F32), limit=4)
    grad_conv, grad_down = call(
        functools.partial(join_kernel, plan), [spot], [total, swapped(total, core_link)],
        [shape((part // 2, 2 * plan.rows), F32), shape((part // 2, 2 * plan.down_rows), F32)],
        [pltpu.VMEM((part, 2 * plan.rows), F32), pltpu.VMEM((part, 2 * plan.down_rows), F32)],
        limit=8,
    )
    return (grad_input.reshape(clip.shape), grad_conv.T, grad_down.T)


def solution(mesh):
    placed = (P("tm", "height", None, None), P(), P(), P("tm", "height", None, None))
    return jax.shard_map(
        body,
        mesh=mesh,
        in_specs=placed,
        out_specs=(P("tm", "height", None, None), P("height", "tm"), P("height", "tm")),
        check_vma=False,
    )
```

```python
import functools
import math

import jax
import jax.numpy as jnp
from jax import lax
from jax.experimental import pallas as pl
from jax.experimental.pallas import tpu as pltpu
from jax.sharding import PartitionSpec as P

F32 = jnp.float32
BF16 = jnp.bfloat16
MIB = 1024 * 1024


def dot(left, right):
    return jnp.dot(left, right, preferred_element_type=F32)


def dot_nt(left, right):
    return lax.dot_general(left, right, (((1,), (1,)), ((), ())), preferred_element_type=F32)


def shifted_rows(value, step, period):
    if step == 0:
        return value
    rows = value.shape[0]
    moved = pltpu.roll(value, (-step) % rows, 0)
    place = lax.broadcasted_iota(jnp.int32, value.shape, 0) % period + step
    return jnp.where(jnp.logical_and(place >= 0, place < period), moved, 0.0)


def channel_of(place, group, core):
    return (place // group * 2 + core) * group + place % group


def one_hot(wanted, chans):
    dims = (wanted.shape[0], chans)
    return (lax.broadcasted_iota(jnp.int32, dims, 1) == wanted).astype(F32).astype(BF16)


def picker(chans, group, core):
    place = lax.broadcasted_iota(jnp.int32, (chans // 2, chans), 0)
    return one_hot(channel_of(place, group, core), chans)


def lay_pair(window, core, own, other, begin=0):
    size = own.shape[0]
    window[pl.ds(pl.multiple_of(begin + size * core, size), size)] = own[...]
    window[pl.ds(pl.multiple_of(begin + size * (1 - core), size), size)] = other[...]


def silu(value):
    return value / (1.0 + jnp.exp(-value))


def halved(lead, axis, index):
    rest = lead[:axis] + lead[axis + 1 :]
    for flat in range(math.prod(rest)):
        spot, left = [], flat
        for extent in reversed(rest):
            spot.insert(0, left % extent)
            left //= extent
        yield tuple(spot), tuple(spot[:axis]) + (index,) + tuple(spot[axis:])


def bit_of(spot_ref, link):
    return lax.shift_right_logical(spot_ref[link[0]], link[1]) & 1


def split_into(send, keep, lead, axis, mine, read):
    for to, where in halved(lead, axis, 1 - mine):
        send[to] = read(where).astype(send.dtype)
    for to, where in halved(lead, axis, mine):
        keep[to] = read(where)


def weights_kernel(plan, spot_ref, weight_ref, down_ref, turned_ref, spread_ref):
    chans, group = plan.chans, plan.group
    part = chans // 2
    core = spot_ref[0] & 1
    place = lax.broadcasted_iota(jnp.int32, (chans, chans), 0)
    order = one_hot(channel_of(place % part, group, place // part), chans)
    pick = picker(chans, group, core)
    for ab in range(9):
        picked = [dot(pick, weight_ref[ab, c * chans : (c + 1) * chans]).astype(BF16) for c in range(3)]
        turned_ref[ab] = dot_nt(order, jnp.concatenate(picked, axis=0)).astype(BF16)
    for k in range(3):
        spread_ref[k * chans : (k + 1) * chans] = down_ref[k].T


def row_terms(plan, even, odd, cells, spread_ref, turned_ref, b):
    chans = plan.chans
    span = cells.shape[0]
    cross = []
    for s in range(5):
        begin = s // 2 * plan.cols
        cross.append(dot((even, odd)[s % 2][:, begin : begin + span], cells).astype(BF16))
    conv, down = [], None
    for a in range(3):
        three = jnp.concatenate(cross[a : a + 3], axis=1)
        conv.append(dot(three, spread_ref[...]))
        term = dot(turned_ref[a * 3 + b], three)
        down = term if down is None else down + term
    return conv, down


def near_kernel(plan, spot_ref, clip_ref, clip_other, first_ref, second_ref, here_ref, here_other, side_ref, side_other,
                spread_ref, turned_ref, even_ref, odd_ref, conv_ref, down_ref, clips, cells, more_cells):
    cols, chans, group = plan.cols, plan.chans, plan.group
    part = chans // 2
    core = spot_ref[0] & 1
    rows = clip_ref.shape[0]
    span = here_ref.shape[0]
    clips[:rows] = first_ref[...] + second_ref[...]
    lay_pair(clips, core, clip_ref, clip_other, rows)
    pick = picker(chans, group, core)
    value = clips[...]
    chosen = dot_nt(pick, silu(value.astype(F32)).astype(BF16))
    steps = lax.broadcasted_iota(jnp.int32, chosen.shape, 1) % cols
    count = 3 * rows // cols // 2
    for c in range(3):
        moved = chosen
        if c != 1:
            moved = pltpu.roll(chosen, (1 - c) % chosen.shape[1], 1)
            moved = jnp.where(steps == (0 if c == 0 else cols - 1), 0.0, moved)
        moved = moved.astype(BF16)
        lanes = slice(c * part, (c + 1) * part)
        for f in range(count):
            to = slice(f * cols, (f + 1) * cols)
            even_ref[lanes, to] = moved[:, 2 * f * cols : (2 * f + 1) * cols]
            odd_ref[lanes, to] = moved[:, (2 * f + 1) * cols : (2 * f + 2) * cols]
    plain = dot_nt(pick, value).astype(BF16)
    halves = [
        jnp.concatenate([plain[:, (2 * f + p) * cols : (2 * f + p + 1) * cols] for f in range(count)], axis=1)
        for p in range(2)
    ]
    lay_pair(cells, core, here_ref, here_other)
    lay_pair(more_cells, core, side_ref, side_other)
    here = cells[...]
    conv, down = row_terms(plan, even_ref, odd_ref, here, spread_ref, turned_ref, 1)
    for a in range(3):
        conv_ref[0, a] = conv[a]
    b = 2 * (spot_ref[1] & 1)
    conv, more = row_terms(plan, even_ref, odd_ref, more_cells[...], spread_ref, turned_ref, b)
    for a in range(3):
        conv_ref[1, a] = conv[a]
    down_ref[...] = down + more
    own = pl.ds(pl.multiple_of(core * part, part), part)
    for k in range(3):
        begin = (1 + k // 2) * cols
        lanes = slice(k * chans, (k + 1) * chans)
        down_ref[own, lanes] = down_ref[own, lanes] + dot(halves[k % 2][:, begin : begin + 2 * span], here)


def far_kernel(plan, spot_ref, here_ref, side_ref, far_ref, far_other, even_ref, odd_ref, conv_ref, down_ref, spread_ref,
               turned_ref, head_ref, *rest):
    outs, (cells, total) = rest[:-2], rest[-2:]
    chans = plan.chans
    part = chans // 2
    core = spot_ref[0] & 1
    odd_row = spot_ref[1] & 1
    lay_pair(cells, core, far_ref, far_other)
    conv, down = row_terms(plan, even_ref, odd_ref, cells[...], spread_ref, turned_ref, 2 - 2 * odd_row)
    down = down_ref[...] + down
    for slot, ref in enumerate((here_ref, side_ref, far_ref)):
        head_ref[slot] = ref[...]
    wide = 3 * part

    def place(a, b, value):
        first = (a * 3 + b) * wide
        begin = first
        while begin < first + wide:
            h = begin // plan.rows
            end = min((h + 1) * plan.rows, first + wide)
            for y in range(2):
                total[(y,) + plan.spot(h) + (slice(begin - h * plan.rows, end - h * plan.rows),)] = value[
                    begin - first : end - first, y * part : (y + 1) * part
                ]
            begin = end

    for a in range(3):
        place(a, 1, conv_ref[0, a])
    for parity in range(2):
        @pl.when(odd_row == parity)
        def _():
            for a in range(3):
                place(a, 2 * parity, conv_ref[1, a])
                place(a, 2 - 2 * parity, conv[a])
    for g in range(3):
        link = plan.orders[g][0]
        begin, end = plan.cuts[g]
        split_into(
            outs[2 * g], outs[2 * g + 1], plan.lead, plan.axis(g, 0), bit_of(spot_ref, link),
            lambda where: total[where + (slice(begin, end),)],
        )
    mine = core == 0
    low, high = down[:part], down[part:]
    for ref, value in ((outs[6], jnp.where(mine, high, low)), (outs[7], jnp.where(mine, low, high))):
        for h in range(math.prod(plan.lead[1:])):
            begin = h * plan.down_rows
            while begin < (h + 1) * plan.down_rows:
                k = begin // part
                end = min((k + 1) * part, (h + 1) * plan.down_rows)
                for y in range(2):
                    ref[(y,) + plan.spot(h) + (slice(begin - h * plan.down_rows, end - h * plan.down_rows),)] = value[
                        begin - k * part : end - k * part, k * chans + y * part : k * chans + (y + 1) * part
                    ].astype(ref.dtype)
                begin = end


def down_split_kernel(plan, spot_ref, keep_ref, got_ref, send, keep):
    split_into(
        send, keep, plan.lead, plan.axis(0, 0), bit_of(spot_ref, plan.orders[0][0]),
        lambda where: keep_ref[where] + got_ref[where].astype(F32),
    )


def fold_kernel(plan, step, spot_ref, *refs):
    extra = 2 if step == 1 else 0
    ins, outs = refs[: 6 + extra], refs[6 + extra :]
    for g in range(3):
        link = plan.orders[g][step]
        axis = plan.axis(g, step)
        mine = bit_of(spot_ref, link)
        held, got = ins[2 * g], ins[2 * g + 1]

        def read(where):
            value = held[where] + got[where].astype(F32)
            if step == 1 and g == 0:
                value = jnp.concatenate([value, ins[6][where] + ins[7][where].astype(F32)], axis=0)
            return value

        lead = plan.lead[step:]
        if step < 3:
            split_into(outs[2 * g], outs[2 * g + 1], lead, axis, mine, read)
        else:
            third = held.shape[-2]
            for to, where in halved(lead, axis, 1 - mine):
                outs[0][to + (slice(g * third, (g + 1) * third),)] = read(where).astype(BF16)
            for to, where in halved(lead, axis, mine):
                outs[1][to + (slice(g * third, (g + 1) * third),)] = read(where)


def late_kernel(plan, step, spot_ref, held, got, send, keep):
    link = plan.orders[0][step]
    split_into(
        send, keep, plan.lead[step:], plan.axis(0, step), bit_of(spot_ref, link),
        lambda where: held[where] + got[where].astype(F32),
    )


def last_kernel(held, got, out):
    out[...] = held[...] + got[...].astype(F32)


def join_kernel(plan, spot_ref, mine_ref, other_ref, conv_ref, down_ref, turned, down_turned):
    core = spot_ref[0] & 1
    group = plan.group
    rows, down_rows = plan.rows, plan.down_rows
    own, other = mine_ref[...], other_ref[...]
    first, second = jnp.where(core == 0, own, other), jnp.where(core == 0, other, own)

    def merged(begin, end):
        pieces = []
        for at in range(begin, end, group):
            pieces += [first[at : at + group], second[at : at + group]]
        return pieces

    cut = plan.cuts[0][1]
    conv = merged(0, cut) + merged(cut + down_rows, rows + down_rows)
    down = merged(cut, cut + down_rows)
    width = own.shape[1] // 2
    for ref, pieces, space in ((conv_ref, conv, turned), (down_ref, down, down_turned)):
        space[...] = jnp.concatenate(pieces, axis=0).T
        ref[...] = space[pl.ds(pl.multiple_of(core * width, width), width)]


def input_kernel(plan, spot_ref, clip_ref, here_ref, here_other, side_ref, side_other, far_ref, far_other, next_ref,
                 down_ref, weight_ref, out_ref, grads):
    cols, chans = plan.cols, plan.chans
    cells = clip_ref.shape[0]
    half = here_ref.shape[0] // cols
    core = spot_ref[0] & 1
    side = 2 * (spot_ref[1] & 1)
    rows = ((here_ref, here_other), (side_ref, side_other), (far_ref, far_other))
    for slot, (own, other) in enumerate(rows):
        following = jnp.where(core == 0, other[...], next_ref[slot])
        every = jnp.concatenate([own[...], following], axis=0)
        here = every[: (half + 1) * cols]
        after = every[cols : (half + 2) * cols]
        even = (dot_nt(after, down_ref[0]) + dot_nt(here, down_ref[2])).astype(BF16)
        odd = dot_nt(after, down_ref[1]).astype(BF16)
        for u in range(half + 1):
            grads[slot, 2 * u * cols : (2 * u + 1) * cols] = even[u * cols : (u + 1) * cols]
            grads[slot, (2 * u + 1) * cols : (2 * u + 2) * cols] = odd[u * cols : (u + 1) * cols]
    acc = [jnp.zeros((cells, chans), F32) for _ in range(3)]
    for a in range(3):
        for slot, b in enumerate((1, side, 2 - side)):
            begin = (2 - a) * cols
            part = grads[slot, begin : begin + cells]
            for c in range(3):
                acc[c] = acc[c] + dot_nt(part, weight_ref[a * 3 + b, c * chans : (c + 1) * chans])
    grad_act = acc[1]
    for c in (0, 2):
        grad_act = grad_act + shifted_rows(acc[c], 1 - c, cols)
    value = clip_ref[...].astype(F32)
    sig = 1.0 / (1.0 + jnp.exp(-value))
    own = grads[0, :cells].astype(F32)
    out_ref[...] = (own + grad_act * (sig * (1.0 + value * (1.0 - sig)))).astype(BF16)


def shape(dims, dtype):
    return jax.ShapeDtypeStruct(dims, dtype)


def call(kernel, scalars, args, outs, scratch=(), us=1, limit=48, after=()):
    vmem, smem = pl.BlockSpec(memory_space=pltpu.VMEM), pl.BlockSpec(memory_space=pltpu.SMEM)
    size = sum(a.size * a.dtype.itemsize for a in args)
    given = len(scalars) + len(args)

    def run(*refs):
        kernel(*refs[:given], *refs[given + len(after) :])

    return pl.pallas_call(
        run,
        out_shape=outs,
        in_specs=[smem] * len(scalars) + [vmem] * len(args) + [pl.BlockSpec(memory_space=pl.ANY)] * len(after),
        out_specs=jax.tree.map(lambda _: vmem, outs),
        scratch_shapes=list(scratch),
        compiler_params=pltpu.CompilerParams(vmem_limit_bytes=limit * MIB),
        cost_estimate=pl.CostEstimate(flops=int(us * 1.15e9), bytes_accessed=size, transcendentals=0),
    )(*scalars, *args, *after)


class Plan:
    def __init__(self, count, cols, chans):
        nbits = count.bit_length() - 1
        self.cols, self.chans = cols, chans
        self.rows, self.down_rows = 27 * chans // count // 2, 3 * chans // count // 2
        self.group = math.gcd(16, math.gcd(self.rows, self.down_rows))
        self.lead = (2,) * (1 + nbits)
        links = [(0, 1)] + [(1, i) for i in range(nbits)]
        self.place = {link: (0 if link[0] == 0 else nbits - link[1]) for link in links}
        tops, tail = links[:3], links[3:]
        self.orders = [tops[g:] + tops[:g] + tail for g in range(3)]
        total = self.rows + self.down_rows
        self.third = total // 3
        cut = self.third - self.down_rows
        self.cuts = [(0, cut), (cut, cut + self.third), (cut + self.third, self.rows)]

    def spot(self, h):
        nbits = len(self.lead) - 1
        return tuple(h >> (nbits - 1 - i) & 1 for i in range(nbits))

    def axis(self, g, step):
        order = self.orders[g]
        return sum(self.place[link] < self.place[order[step]] for link in order[step + 1 :])


def swapped(value, link):
    axis = ("tm", "height")[link[0]]
    return lax.ppermute(value, axis, [(i, i ^ (1 << link[1])) for i in range(lax.axis_size(axis))])


def body(clip, conv_weight, down_weight, grad_out):
    nframes, nrows, ncols, chans = clip.shape
    half = grad_out.shape[0]
    cells, span = nframes * ncols, half * ncols
    tm_count, count = lax.axis_size("tm"), lax.axis_size("height")
    plan = Plan(count, ncols, chans)
    spot = jnp.stack([lax.axis_index("tm"), lax.axis_index("height")]).astype(jnp.int32)
    mine = grad_out.reshape(span, chans)
    flat = clip.reshape(cells, chans)
    weight = conv_weight.reshape(9, 3 * chans, chans)
    core_link = (0, 0)
    part = chans // 2
    wide = 3 * part
    lead = plan.lead
    pair = 2 * span

    side = swapped(mine, (1, 0))
    here_other = swapped(mine, core_link)
    clip_other = swapped(flat, core_link)
    first = lax.ppermute(flat, "tm", [(i, i + 1) for i in range(1, tm_count - 1, 2)])
    second = lax.ppermute(flat, "tm", [(i, i + 2) for i in range(1, tm_count - 2, 2)])
    far = lax.ppermute(
        side, "height", [(i, i + (2 if i % 2 == 0 else -2)) for i in range(count) if 0 <= i + (2 if i % 2 == 0 else -2) < count]
    )
    side_other, far_other = swapped(side, core_link), swapped(far, core_link)

    turned, spread = call(
        functools.partial(weights_kernel, plan), [spot], [weight, down_weight],
        [shape((9, chans, wide), BF16), shape((wide * 2, chans), BF16)], us=2, limit=16,
    )
    even, odd, conv_near, down_near = call(
        functools.partial(near_kernel, plan), [spot],
        [flat, clip_other, first, second, mine, here_other, side, side_other, spread, turned],
        [
            shape((wide, 3 * cells // 2), BF16), shape((wide, 3 * cells // 2), BF16),
            shape((2, 3, wide, chans), F32), shape((chans, 3 * chans), F32),
        ],
        [pltpu.VMEM((3 * cells, chans), BF16), pltpu.VMEM((pair, chans), BF16), pltpu.VMEM((pair, chans), BF16)],
        us=5, limit=24,
    )
    outs = [shape((3, span, chans), BF16)]
    for begin, end in plan.cuts:
        outs += [shape(lead[1:] + (end - begin, part), BF16), shape(lead[1:] + (end - begin, part), F32)]
    down_dims = lead + (plan.down_rows, part)
    outs += [shape(down_dims, BF16), shape(down_dims, F32)]
    result = call(
        functools.partial(far_kernel, plan), [spot],
        [mine, side, far, far_other, even, odd, conv_near, down_near, spread, turned],
        outs,
        [pltpu.VMEM((pair, chans), BF16), pltpu.VMEM(lead + (plan.rows, part), F32)],
        us=4, limit=24,
    )
    head, down_send, down_keep = result[0], result[7], result[8]
    held = []
    for g in range(3):
        held += [result[2 + 2 * g], swapped(result[1 + 2 * g], plan.orders[g][0])]
    send, keep = call(
        functools.partial(down_split_kernel, plan), [spot], [down_keep, swapped(down_send, core_link)],
        [shape(down_dims[1:], BF16), shape(down_dims[1:], F32)], limit=8,
    )
    held += [keep, swapped(send, plan.orders[0][0])]
    following = lax.ppermute(head, "tm", [(i + 1, i) for i in range(1, tm_count - 1, 2)])
    grad_input = call(
        functools.partial(input_kernel, plan), [spot],
        [flat, mine, here_other, side, side_other, far, far_other, following, down_weight, weight],
        shape((cells, chans), BF16),
        [pltpu.VMEM((3, (2 * half + 2) * ncols, chans), BF16)],
        us=4, limit=24,
    )
    for step in (1, 2):
        dims = lead[step + 1 :] + (plan.third, part)
        result = call(
            functools.partial(fold_kernel, plan, step), [spot], held,
            [shape(dims, BF16), shape(dims, F32)] * 3, limit=16,
        )
        held = []
        for g in range(3):
            held += [result[2 * g + 1], swapped(result[2 * g], plan.orders[g][step])]
    for step in range(3, len(lead)):
        dims = lead[step + 1 :] + (3 * plan.third, part)
        kernel = fold_kernel if step == 3 else late_kernel
        send, keep = call(
            functools.partial(kernel, plan, step), [spot], held, [shape(dims, BF16), shape(dims, F32)], limit=8,
            after=[grad_input] if step == 3 else (),
        )
        held = [keep, swapped(send, plan.orders[0][step])]
    total = call(last_kernel, [], held, shape((3 * plan.third, part), F32), limit=4)
    grad_conv, grad_down = call(
        functools.partial(join_kernel, plan), [spot], [total, swapped(total, core_link)],
        [shape((part // 2, 2 * plan.rows), F32), shape((part // 2, 2 * plan.down_rows), F32)],
        [pltpu.VMEM((part, 2 * plan.rows), F32), pltpu.VMEM((part, 2 * plan.down_rows), F32)],
        limit=8,
    )
    return (grad_input.reshape(clip.shape), grad_conv.T, grad_down.T)


def solution(mesh):
    placed = (P("tm", "height", None, None), P(), P(), P("tm", "height", None, None))
    return jax.shard_map(
        body,
        mesh=mesh,
        in_specs=placed,
        out_specs=(P("tm", "height", None, None), P("height", "tm"), P("height", "tm")),
        check_vma=False,
    )
```

```python
import functools
import math

import jax
import jax.numpy as jnp
from jax import lax
from jax.experimental import pallas as pl
from jax.experimental.pallas import tpu as pltpu
from jax.sharding import PartitionSpec as P

F32 = jnp.float32
BF16 = jnp.bfloat16
MIB = 1024 * 1024


def dot(left, right):
    return jnp.dot(left, right, preferred_element_type=F32)


def dot_nt(left, right):
    return lax.dot_general(left, right, (((1,), (1,)), ((), ())), preferred_element_type=F32)


def shifted_rows(value, step, period):
    if step == 0:
        return value
    rows = value.shape[0]
    moved = pltpu.roll(value, (-step) % rows, 0)
    place = lax.broadcasted_iota(jnp.int32, value.shape, 0) % period + step
    return jnp.where(jnp.logical_and(place >= 0, place < period), moved, 0.0)


def channel_of(place, group, core):
    return (place // group * 2 + core) * group + place % group


def one_hot(wanted, chans):
    dims = (wanted.shape[0], chans)
    return (lax.broadcasted_iota(jnp.int32, dims, 1) == wanted).astype(F32).astype(BF16)


def picker(chans, group, core):
    place = lax.broadcasted_iota(jnp.int32, (chans // 2, chans), 0)
    return one_hot(channel_of(place, group, core), chans)


def lay_pair(window, core, own, other, begin=0):
    size = own.shape[0]
    window[pl.ds(pl.multiple_of(begin + size * core, size), size)] = own[...]
    window[pl.ds(pl.multiple_of(begin + size * (1 - core), size), size)] = other[...]


def silu(value):
    return value / (1.0 + jnp.exp(-value))


def halved(lead, axis, index):
    rest = lead[:axis] + lead[axis + 1 :]
    for flat in range(math.prod(rest)):
        spot, left = [], flat
        for extent in reversed(rest):
            spot.insert(0, left % extent)
            left //= extent
        yield tuple(spot), tuple(spot[:axis]) + (index,) + tuple(spot[axis:])


def bit_of(spot_ref, link):
    return lax.shift_right_logical(spot_ref[link[0]], link[1]) & 1


def split_into(send, keep, lead, axis, mine, read):
    for to, where in halved(lead, axis, 1 - mine):
        send[to] = read(where).astype(send.dtype)
    for to, where in halved(lead, axis, mine):
        keep[to] = read(where)


def weights_kernel(plan, spot_ref, weight_ref, down_ref, turned_ref, spread_ref, weights, downs, sems):
    chans = plan.chans
    core = spot_ref[0] & 1
    copies = [pltpu.make_async_copy(down_ref, downs, sems.at[9])]
    copies += [pltpu.make_async_copy(weight_ref.at[ab, :, :, core], weights.at[ab], sems.at[ab]) for ab in range(9)]
    for copy in copies:
        copy.start()
    same = one_hot(lax.broadcasted_iota(jnp.int32, (chans, chans), 0), chans)
    copies[0].wait()
    for k in range(3):
        spread_ref[k * chans : (k + 1) * chans] = dot_nt(same, downs[k]).astype(BF16)
    for ab in range(9):
        copies[ab + 1].wait()
        turned_ref[ab] = dot_nt(same, weights[ab].reshape(3 * chans // 2, chans)).astype(BF16)


def row_terms(plan, even, odd, cells, spread_ref, turned_ref, b, conv_ref):
    chans = plan.chans
    span = cells.shape[0]
    cross = []
    for s in range(5):
        begin = s // 2 * plan.cols
        cross.append(dot((even, odd)[s % 2][:, begin : begin + span], cells).astype(BF16))
    down = None
    for a in range(3):
        three = jnp.concatenate(cross[a : a + 3], axis=1)
        conv_ref[a] = dot(three, spread_ref[...])
        term = dot(turned_ref[a * 3 + b], three)
        down = term if down is None else down + term
    return down


def own_kernel(plan, spot_ref, clip_ref, clip_other, first_ref, second_ref, here_ref, here_other, spread_ref, turned_ref,
               even_ref, odd_ref, conv_ref, sum_ref, plus_ref, clips, cells):
    cols, chans = plan.cols, plan.chans
    part = chans // 2
    core = spot_ref[0] & 1
    rows = clip_ref.shape[0]
    clips[:rows] = first_ref[...] + second_ref[...]
    lay_pair(clips, core, clip_ref, clip_other, rows)
    lay_pair(cells, core, here_ref, here_other)
    pick = picker(chans, plan.group, core)
    plain = dot_nt(pick, clips[...])
    chosen = silu(plain).astype(BF16).astype(F32)
    plain = plain.astype(BF16)
    steps = lax.broadcasted_iota(jnp.int32, chosen.shape, 1) % cols
    count = 3 * rows // cols // 2
    for c in range(3):
        moved = chosen
        if c != 1:
            moved = pltpu.roll(chosen, (1 - c) % chosen.shape[1], 1)
            moved = jnp.where(steps == (0 if c == 0 else cols - 1), 0.0, moved)
        moved = moved.astype(BF16)
        lanes = slice(c * part, (c + 1) * part)
        for f in range(count):
            to = slice(f * cols, (f + 1) * cols)
            even_ref[lanes, to] = moved[:, 2 * f * cols : (2 * f + 1) * cols]
            odd_ref[lanes, to] = moved[:, (2 * f + 1) * cols : (2 * f + 2) * cols]
    here = cells[...]
    for k in range(3):
        halves = [plain[:, (2 * f + k % 2) * cols : (2 * f + k % 2 + 1) * cols] for f in range(count)]
        begin = 1 + k // 2
        frames = jnp.concatenate(halves[begin : begin + here.shape[0] // cols], axis=1)
        plus_ref[:, k * chans : (k + 1) * chans] = dot(frames, here)
    sum_ref[...] = row_terms(plan, even_ref, odd_ref, here, spread_ref, turned_ref, 1, conv_ref)


def side_kernel(plan, spot_ref, side_ref, side_other, even_ref, odd_ref, spread_ref, turned_ref, conv_ref, sum_ref, cells):
    lay_pair(cells, spot_ref[0] & 1, side_ref, side_other)
    b = 2 * (spot_ref[1] & 1)
    sum_ref[...] = row_terms(plan, even_ref, odd_ref, cells[...], spread_ref, turned_ref, b, conv_ref)


def far_kernel(plan, spot_ref, here_ref, side_ref, far_ref, far_other, even_ref, odd_ref, own_conv, own_sum, plus_ref, side_conv,
               side_sum, spread_ref, turned_ref, head_ref, *rest):
    outs, (cells, conv, total) = rest[:-3], rest[-3:]
    chans = plan.chans
    part = chans // 2
    core = spot_ref[0] & 1
    odd_row = spot_ref[1] & 1
    lay_pair(cells, core, far_ref, far_other)
    down = row_terms(plan, even_ref, odd_ref, cells[...], spread_ref, turned_ref, 2 - 2 * odd_row, conv)
    down = own_sum[...] + side_sum[...] + down
    for slot, ref in enumerate((here_ref, side_ref, far_ref)):
        head_ref[slot] = ref[...]
    wide = 3 * part

    def place(a, b, value):
        first = (a * 3 + b) * wide
        begin = first
        while begin < first + wide:
            h = begin // plan.rows
            end = min((h + 1) * plan.rows, first + wide)
            for y in range(2):
                total[(y,) + plan.spot(h) + (slice(begin - h * plan.rows, end - h * plan.rows),)] = value[
                    begin - first : end - first, y * part : (y + 1) * part
                ]
            begin = end

    for a in range(3):
        place(a, 1, own_conv[a])
    for parity in range(2):
        @pl.when(odd_row == parity)
        def _():
            for a in range(3):
                place(a, 2 * parity, side_conv[a])
                place(a, 2 - 2 * parity, conv[a])
    for g in range(3):
        link = plan.orders[g][0]
        begin, end = plan.cuts[g]
        split_into(
            outs[2 * g], outs[2 * g + 1], plan.lead, plan.axis(g, 0), bit_of(spot_ref, link),
            lambda where: total[where + (slice(begin, end),)],
        )
    mine = core == 0
    pairs = range(0, chans, 2 * plan.group)
    low = jnp.concatenate([down[i : i + plan.group] for i in pairs], axis=0)
    high = jnp.concatenate([down[i + plan.group : i + 2 * plan.group] for i in pairs], axis=0)
    keep = jnp.where(mine, low, high) + plus_ref[...]
    for ref, value in ((outs[6], jnp.where(mine, high, low)), (outs[7], keep)):
        for h in range(math.prod(plan.lead[1:])):
            begin = h * plan.down_rows
            while begin < (h + 1) * plan.down_rows:
                k = begin // part
                end = min((k + 1) * part, (h + 1) * plan.down_rows)
                for y in range(2):
                    ref[(y,) + plan.spot(h) + (slice(begin - h * plan.down_rows, end - h * plan.down_rows),)] = value[
                        begin - k * part : end - k * part, k * chans + y * part : k * chans + (y + 1) * part
                    ].astype(ref.dtype)
                begin = end


def fold_kernel(plan, step, spot_ref, *refs):
    extra = 2 if step == 1 else 0
    ins, outs = refs[: 6 + extra], refs[6 + extra :]
    at = 0
    for g in range(3):
        link = plan.orders[g][step]
        axis = plan.axis(g, step)
        mine = bit_of(spot_ref, link)
        held, got = ins[2 * g], ins[2 * g + 1]

        def read(where):
            value = held[where] + got[where].astype(F32)
            if extra and g == 0:
                value = jnp.concatenate([value, ins[6][where] + ins[7][where].astype(F32)], axis=0)
            return value

        lead = plan.lead[step:]
        if step < 3:
            split_into(outs[2 * g], outs[2 * g + 1], lead, axis, mine, read)
        else:
            rows = slice(at, at + held.shape[-2])
            at = at + held.shape[-2]
            for to, where in halved(lead, axis, 1 - mine):
                outs[0][to + (rows,)] = read(where).astype(BF16)
            for to, where in halved(lead, axis, mine):
                outs[1][to + (rows,)] = read(where)


def single_kernel(plan, step, spot_ref, held, got, send, keep):
    split_into(
        send, keep, plan.lead[step:], plan.axis(0, step), bit_of(spot_ref, plan.orders[0][step]),
        lambda where: held[where] + got[where].astype(F32),
    )


def join_kernel(plan, spot_ref, held, got, held_other, got_other, conv_ref, down_ref, turned, down_turned):
    core = spot_ref[0] & 1
    group = plan.group
    rows, down_rows = plan.rows, plan.down_rows
    own = held[...] + got[...].astype(F32)
    other = held_other[...] + got_other[...].astype(F32)
    first, second = jnp.where(core == 0, own, other), jnp.where(core == 0, other, own)

    def merged(begin, end):
        pieces = []
        for at in range(begin, end, group):
            pieces += [first[at : at + group], second[at : at + group]]
        return pieces

    cut = plan.cuts[0][1]
    conv = merged(0, cut) + merged(cut + down_rows, rows + down_rows)
    down = merged(cut, cut + down_rows)
    width = own.shape[1] // 2
    for ref, pieces, space in ((conv_ref, conv, turned), (down_ref, down, down_turned)):
        space[...] = jnp.concatenate(pieces, axis=0).T
        ref[...] = space[pl.ds(pl.multiple_of(core * width, width), width)]


def input_kernel(plan, spot_ref, clip_ref, here_ref, here_other, side_ref, side_other, far_ref, far_other, next_ref,
                 down_ref, weight_ref, out_ref, done_ref, grads):
    cols, chans = plan.cols, plan.chans
    cells = clip_ref.shape[0]
    span = side_ref.shape[0]
    half = span // cols
    core = spot_ref[0] & 1
    side = 2 * (spot_ref[1] & 1)
    rows = ((here_ref, here_other), (side_ref, side_other), (far_ref, far_other))
    for slot, (own, other) in enumerate(rows):
        following = jnp.where(core == 0, other[...], next_ref[slot])
        every = jnp.concatenate([own[...], following], axis=0)
        here = every[: (half + 1) * cols]
        after = every[cols : (half + 2) * cols]
        even = (dot_nt(after, down_ref[0]) + dot_nt(here, down_ref[2])).astype(BF16)
        odd = dot_nt(after, down_ref[1]).astype(BF16)
        for u in range(half + 1):
            grads[slot, 2 * u * cols : (2 * u + 1) * cols] = even[u * cols : (u + 1) * cols]
            grads[slot, (2 * u + 1) * cols : (2 * u + 2) * cols] = odd[u * cols : (u + 1) * cols]
    acc = [jnp.zeros((cells, chans), F32) for _ in range(3)]
    for a in range(3):
        for slot, b in enumerate((1, side, 2 - side)):
            begin = (2 - a) * cols
            part = grads[slot, begin : begin + cells]
            for c in range(3):
                acc[c] = acc[c] + dot_nt(part, weight_ref[a * 3 + b, c * chans : (c + 1) * chans])
    grad_act = acc[1]
    for c in (0, 2):
        grad_act = grad_act + shifted_rows(acc[c], 1 - c, cols)
    value = clip_ref[...].astype(F32)
    sig = 1.0 / (1.0 + jnp.exp(-value))
    own = grads[0, :cells].astype(F32)
    out_ref[...] = (own + grad_act * (sig * (1.0 + value * (1.0 - sig)))).astype(BF16)
    done_ref[...] = jnp.zeros_like(done_ref)


def shape(dims, dtype):
    return jax.ShapeDtypeStruct(dims, dtype)


def call(kernel, scalars, args, outs, scratch=(), us=1, limit=48, after=(), left=0):
    vmem, smem = pl.BlockSpec(memory_space=pltpu.VMEM), pl.BlockSpec(memory_space=pltpu.SMEM)
    hbm = pl.BlockSpec(memory_space=pltpu.HBM)
    args = [pltpu.with_memory_space_constraint(a, pltpu.HBM) for a in args[:left]] + list(args[left:])
    after = list(after)
    size = sum(a.size * a.dtype.itemsize for a in args)
    given = len(scalars) + len(args)

    def run(*refs):
        kernel(*refs[:given], *refs[given + len(after) :])

    return pl.pallas_call(
        run,
        out_shape=outs,
        in_specs=[smem] * len(scalars) + [hbm] * left + [vmem] * (len(args) - left) + [vmem] * len(after),
        out_specs=jax.tree.map(lambda _: vmem, outs),
        scratch_shapes=list(scratch),
        compiler_params=pltpu.CompilerParams(vmem_limit_bytes=limit * MIB),
        cost_estimate=pl.CostEstimate(flops=int(us * 1.15e9), bytes_accessed=size, transcendentals=0),
    )(*scalars, *args, *after)


class Plan:
    def __init__(self, count, cols, chans):
        nbits = count.bit_length() - 1
        self.cols, self.chans = cols, chans
        self.rows, self.down_rows = 27 * chans // count // 2, 3 * chans // count // 2
        self.group = math.gcd(16, math.gcd(self.rows, self.down_rows))
        self.lead = (2,) * (1 + nbits)
        links = [(0, 1)] + [(1, i) for i in range(nbits)]
        self.place = {link: (0 if link[0] == 0 else nbits - link[1]) for link in links}
        tops, tail = links[:3], links[3:]
        self.orders = [tops[g:] + tops[:g] + tail for g in range(3)]
        third = (self.rows + self.down_rows) // 3
        cut = third - self.down_rows
        self.cuts = [(0, cut), (cut, cut + third), (cut + third, self.rows)]

    def spot(self, h):
        nbits = len(self.lead) - 1
        return tuple(h >> (nbits - 1 - i) & 1 for i in range(nbits))

    def axis(self, g, step):
        order = self.orders[g]
        return sum(self.place[link] < self.place[order[step]] for link in order[step + 1 :])


def swapped(value, link):
    axis = ("tm", "height")[link[0]]
    return lax.ppermute(value, axis, [(i, i ^ (1 << link[1])) for i in range(lax.axis_size(axis))])


def body(clip, conv_weight, down_weight, grad_out):
    nframes, nrows, ncols, chans = clip.shape
    half = grad_out.shape[0]
    cells, span = nframes * ncols, half * ncols
    tm_count, count = lax.axis_size("tm"), lax.axis_size("height")
    plan = Plan(count, ncols, chans)
    spot = jnp.stack([lax.axis_index("tm"), lax.axis_index("height")]).astype(jnp.int32)
    mine = grad_out.reshape(span, chans)
    flat = clip.reshape(cells, chans)
    weight = conv_weight.reshape(9, 3 * chans, chans)
    core_link = (0, 0)
    part = chans // 2
    wide = 3 * part
    lead = plan.lead
    pair = 2 * span

    side = swapped(mine, (1, 0))
    here_other = swapped(mine, core_link)
    clip_other = swapped(flat, core_link)
    first = lax.ppermute(flat, "tm", [(i, i + 1) for i in range(1, tm_count - 1, 2)])
    second = lax.ppermute(flat, "tm", [(i, i + 2) for i in range(1, tm_count - 2, 2)])
    listed = (9, 3, part // plan.group, 2, plan.group, chans)
    turned, spread = call(
        functools.partial(weights_kernel, plan), [spot], [weight.reshape(listed), down_weight],
        [shape((9, chans, wide), BF16), shape((2 * wide, chans), BF16)],
        [pltpu.VMEM(listed[:3] + listed[4:], BF16), pltpu.VMEM(down_weight.shape, BF16), pltpu.SemaphoreType.DMA((10,))],
        us=3, limit=16, left=2,
    )
    far = lax.ppermute(
        side, "height", [(i, i + (2 if i % 2 == 0 else -2)) for i in range(count) if 0 <= i + (2 if i % 2 == 0 else -2) < count]
    )
    side_other = swapped(side, core_link)

    terms = [shape((3, wide, chans), F32), shape((chans, 3 * chans), F32)]
    even, odd, own_conv, own_sum, plus = call(
        functools.partial(own_kernel, plan), [spot],
        [flat, clip_other, first, second, mine, here_other, spread, turned],
        [shape((wide, 3 * cells // 2), BF16), shape((wide, 3 * cells // 2), BF16), *terms, shape((part, 3 * chans), F32)],
        [pltpu.VMEM((3 * cells, chans), BF16), pltpu.VMEM((pair, chans), BF16)], us=3, limit=20,
    )
    far, plus = lax.optimization_barrier((far, plus))
    far_other = swapped(far, core_link)
    side_conv, side_sum = call(
        functools.partial(side_kernel, plan), [spot], [side, side_other, even, odd, spread, turned], terms,
        [pltpu.VMEM((pair, chans), BF16)], us=2, limit=20,
    )
    outs = [shape((3, span, chans), BF16)]
    for begin, end in plan.cuts:
        outs += [shape(lead[1:] + (end - begin, part), BF16), shape(lead[1:] + (end - begin, part), F32)]
    down_dims = lead + (plan.down_rows, part)
    outs += [shape(down_dims, BF16), shape(down_dims, F32)]
    result = call(
        functools.partial(far_kernel, plan), [spot],
        [mine, side, far, far_other, even, odd, own_conv, own_sum, plus, side_conv, side_sum, spread, turned], outs,
        [pltpu.VMEM((pair, chans), BF16), pltpu.VMEM((3, wide, chans), F32), pltpu.VMEM(lead + (plan.rows, part), F32)],
        us=3, limit=20,
    )
    head = result[0]
    held = []
    for g in range(3):
        held += [result[2 + 2 * g], swapped(result[1 + 2 * g], plan.orders[g][0])]
    send, keep = call(
        functools.partial(single_kernel, plan, 0), [spot], [result[8], swapped(result[7], core_link)],
        [shape(down_dims[1:], BF16), shape(down_dims[1:], F32)], limit=8,
    )
    down_held = [keep, swapped(send, plan.orders[0][0])]
    following = lax.ppermute(head, "tm", [(i + 1, i) for i in range(1, tm_count - 1, 2)])
    grad_input, done = call(
        functools.partial(input_kernel, plan), [spot],
        [flat, mine, here_other, side, side_other, far, far_other, following, down_weight, weight],
        [shape((cells, chans), BF16), shape((8, part), F32)],
        [pltpu.VMEM((3, (2 * half + 2) * ncols, chans), BF16)],
        us=4, limit=24,
    )
    for step in (1, 2):
        outs = []
        for g in range(3):
            rows = plan.cuts[g][1] - plan.cuts[g][0] + (plan.down_rows if g == 0 else 0)
            outs += [shape(lead[step + 1 :] + (rows, part), BF16), shape(lead[step + 1 :] + (rows, part), F32)]
        extra = down_held if step == 1 else []
        result = call(functools.partial(fold_kernel, plan, step), [spot], held + extra, outs, limit=12)
        held = []
        for g in range(3):
            held += [result[2 * g + 1], swapped(result[2 * g], plan.orders[g][step])]
    for step in range(3, len(lead)):
        dims = lead[step + 1 :] + (plan.rows + plan.down_rows, part)
        kernel = fold_kernel if step == 3 else single_kernel
        send, keep = call(
            functools.partial(kernel, plan, step), [spot], held, [shape(dims, BF16), shape(dims, F32)], limit=8,
            after=[done] if step == 3 else (),
        )
        held = [keep, swapped(send, plan.orders[0][step])]
    grad_conv, grad_down = call(
        functools.partial(join_kernel, plan), [spot], held + [swapped(v, core_link) for v in held],
        [shape((part // 2, 2 * plan.rows), F32), shape((part // 2, 2 * plan.down_rows), F32)],
        [pltpu.VMEM((part, 2 * plan.rows), F32), pltpu.VMEM((part, 2 * plan.down_rows), F32)],
        limit=8,
    )
    return (grad_input.reshape(clip.shape), grad_conv.T, grad_down.T)


def solution(mesh):
    placed = (P("tm", "height", None, None), P(), P(), P("tm", "height", None, None))
    return jax.shard_map(
        body,
        mesh=mesh,
        in_specs=placed,
        out_specs=(P("tm", "height", None, None), P("height", "tm"), P("height", "tm")),
        check_vma=False,
    )
```

```python
import functools
import math

import jax
import jax.numpy as jnp
from jax import lax
from jax.experimental import pallas as pl
from jax.experimental.pallas import tpu as pltpu
from jax.sharding import PartitionSpec as P

F32 = jnp.float32
BF16 = jnp.bfloat16
MIB = 1024 * 1024


def dot(left, right):
    return jnp.dot(left, right, preferred_element_type=F32)


def dot_nt(left, right):
    return lax.dot_general(left, right, (((1,), (1,)), ((), ())), preferred_element_type=F32)


def shifted_rows(value, step, period):
    if step == 0:
        return value
    rows = value.shape[0]
    moved = pltpu.roll(value, (-step) % rows, 0)
    place = lax.broadcasted_iota(jnp.int32, value.shape, 0) % period + step
    return jnp.where(jnp.logical_and(place >= 0, place < period), moved, 0.0)


def channel_of(place, group, core):
    return (place // group * 2 + core) * group + place % group


def one_hot(wanted, chans):
    dims = (wanted.shape[0], chans)
    return (lax.broadcasted_iota(jnp.int32, dims, 1) == wanted).astype(F32).astype(BF16)


def picker(chans, group, core):
    place = lax.broadcasted_iota(jnp.int32, (chans // 2, chans), 0)
    return one_hot(channel_of(place, group, core), chans)


def lay_pair(window, core, own, other, begin=0):
    size = own.shape[0]
    window[pl.ds(pl.multiple_of(begin + size * core, size), size)] = own[...]
    window[pl.ds(pl.multiple_of(begin + size * (1 - core), size), size)] = other[...]


def silu(value):
    return value / (1.0 + jnp.exp(-value))


def halved(lead, axis, index):
    rest = lead[:axis] + lead[axis + 1 :]
    for flat in range(math.prod(rest)):
        spot, left = [], flat
        for extent in reversed(rest):
            spot.insert(0, left % extent)
            left //= extent
        yield tuple(spot), tuple(spot[:axis]) + (index,) + tuple(spot[axis:])


def bit_of(spot_ref, link):
    return lax.shift_right_logical(spot_ref[link[0]], link[1]) & 1


def split_into(send, keep, lead, axis, mine, read):
    for to, where in halved(lead, axis, 1 - mine):
        send[to] = read(where).astype(send.dtype)
    for to, where in halved(lead, axis, mine):
        keep[to] = read(where)


def weights_kernel(plan, spot_ref, weight_ref, down_ref, turned_ref, spread_ref, weights, downs, sems):
    chans = plan.chans
    core = spot_ref[0] & 1
    copies = [pltpu.make_async_copy(down_ref, downs, sems.at[9])]
    copies += [pltpu.make_async_copy(weight_ref.at[ab, :, :, core], weights.at[ab], sems.at[ab]) for ab in range(9)]
    for copy in copies:
        copy.start()
    same = one_hot(lax.broadcasted_iota(jnp.int32, (chans, chans), 0), chans)
    copies[0].wait()
    for k in range(3):
        spread_ref[k * chans : (k + 1) * chans] = dot_nt(same, downs[k]).astype(BF16)
    for ab in range(9):
        copies[ab + 1].wait()
        block = weights[ab].reshape(3 * chans // 2, chans)
        turned_ref[ab] = block.T if ab % 2 else dot_nt(same, block).astype(BF16)


def row_terms(plan, even, odd, cells, spread_ref, turned_ref, b, conv_ref):
    chans = plan.chans
    span = cells.shape[0]
    cross = []
    for s in range(5):
        begin = s // 2 * plan.cols
        cross.append(dot((even, odd)[s % 2][:, begin : begin + span], cells).astype(BF16))
    down = None
    for a in range(3):
        three = jnp.concatenate(cross[a : a + 3], axis=1)
        conv_ref[a] = dot(three, spread_ref[...])
        term = dot(turned_ref[a * 3 + b], three)
        down = term if down is None else down + term
    return down


def own_kernel(plan, spot_ref, clip_ref, clip_other, first_ref, second_ref, here_ref, here_other, spread_ref, turned_ref,
               even_ref, odd_ref, conv_ref, sum_ref, plus_ref, clips, cells):
    cols, chans = plan.cols, plan.chans
    part = chans // 2
    core = spot_ref[0] & 1
    rows = clip_ref.shape[0]
    clips[:rows] = first_ref[...] + second_ref[...]
    lay_pair(clips, core, clip_ref, clip_other, rows)
    lay_pair(cells, core, here_ref, here_other)
    pick = picker(chans, plan.group, core)
    plain = dot_nt(pick, clips[...])
    chosen = silu(plain).astype(BF16).astype(F32)
    plain = plain.astype(BF16)
    steps = lax.broadcasted_iota(jnp.int32, chosen.shape, 1) % cols
    count = 3 * rows // cols // 2
    for c in range(3):
        moved = chosen
        if c != 1:
            moved = pltpu.roll(chosen, (1 - c) % chosen.shape[1], 1)
            moved = jnp.where(steps == (0 if c == 0 else cols - 1), 0.0, moved)
        moved = moved.astype(BF16)
        lanes = slice(c * part, (c + 1) * part)
        for f in range(count):
            to = slice(f * cols, (f + 1) * cols)
            even_ref[lanes, to] = moved[:, 2 * f * cols : (2 * f + 1) * cols]
            odd_ref[lanes, to] = moved[:, (2 * f + 1) * cols : (2 * f + 2) * cols]
    here = cells[...]
    for k in range(3):
        halves = [plain[:, (2 * f + k % 2) * cols : (2 * f + k % 2 + 1) * cols] for f in range(count)]
        begin = 1 + k // 2
        frames = jnp.concatenate(halves[begin : begin + here.shape[0] // cols], axis=1)
        plus_ref[:, k * chans : (k + 1) * chans] = dot(frames, here)
    sum_ref[...] = row_terms(plan, even_ref, odd_ref, here, spread_ref, turned_ref, 1, conv_ref)


def side_kernel(plan, spot_ref, side_ref, side_other, even_ref, odd_ref, spread_ref, turned_ref, conv_ref, sum_ref, cells):
    lay_pair(cells, spot_ref[0] & 1, side_ref, side_other)
    b = 2 * (spot_ref[1] & 1)
    sum_ref[...] = row_terms(plan, even_ref, odd_ref, cells[...], spread_ref, turned_ref, b, conv_ref)


def far_kernel(plan, spot_ref, here_ref, side_ref, far_ref, far_other, even_ref, odd_ref, own_conv, own_sum, plus_ref, side_conv,
               side_sum, spread_ref, turned_ref, head_ref, *rest):
    outs, (cells, conv, total) = rest[:-3], rest[-3:]
    chans = plan.chans
    part = chans // 2
    core = spot_ref[0] & 1
    odd_row = spot_ref[1] & 1
    lay_pair(cells, core, far_ref, far_other)
    down = row_terms(plan, even_ref, odd_ref, cells[...], spread_ref, turned_ref, 2 - 2 * odd_row, conv)
    down = own_sum[...] + side_sum[...] + down
    for slot, ref in enumerate((here_ref, side_ref, far_ref)):
        head_ref[slot] = ref[...]
    wide = 3 * part

    def place(a, b, value):
        first = (a * 3 + b) * wide
        begin = first
        while begin < first + wide:
            h = begin // plan.rows
            end = min((h + 1) * plan.rows, first + wide)
            for y in range(2):
                total[(y,) + plan.spot(h) + (slice(begin - h * plan.rows, end - h * plan.rows),)] = value[
                    begin - first : end - first, y * part : (y + 1) * part
                ]
            begin = end

    for a in range(3):
        place(a, 1, own_conv[a])
    for parity in range(2):
        @pl.when(odd_row == parity)
        def _():
            for a in range(3):
                place(a, 2 * parity, side_conv[a])
                place(a, 2 - 2 * parity, conv[a])
    for g in range(3):
        link = plan.orders[g][0]
        begin, end = plan.cuts[g]
        split_into(
            outs[2 * g], outs[2 * g + 1], plan.lead, plan.axis(g, 0), bit_of(spot_ref, link),
            lambda where: total[where + (slice(begin, end),)],
        )
    mine = core == 0
    pairs = range(0, chans, 2 * plan.group)
    low = jnp.concatenate([down[i : i + plan.group] for i in pairs], axis=0)
    high = jnp.concatenate([down[i + plan.group : i + 2 * plan.group] for i in pairs], axis=0)
    keep = jnp.where(mine, low, high) + plus_ref[...]
    for ref, value in ((outs[6], jnp.where(mine, high, low)), (outs[7], keep)):
        for h in range(math.prod(plan.lead[1:])):
            begin = h * plan.down_rows
            while begin < (h + 1) * plan.down_rows:
                k = begin // part
                end = min((k + 1) * part, (h + 1) * plan.down_rows)
                for y in range(2):
                    ref[(y,) + plan.spot(h) + (slice(begin - h * plan.down_rows, end - h * plan.down_rows),)] = value[
                        begin - k * part : end - k * part, k * chans + y * part : k * chans + (y + 1) * part
                    ].astype(ref.dtype)
                begin = end


def fold_kernel(plan, step, spot_ref, *refs):
    extra = 2 if step == 1 else 0
    ins, outs = refs[: 6 + extra], refs[6 + extra :]
    at = 0
    for g in range(3):
        link = plan.orders[g][step]
        axis = plan.axis(g, step)
        mine = bit_of(spot_ref, link)
        held, got = ins[2 * g], ins[2 * g + 1]

        def read(where):
            value = held[where] + got[where].astype(F32)
            if extra and g == 0:
                value = jnp.concatenate([value, ins[6][where] + ins[7][where].astype(F32)], axis=0)
            return value

        lead = plan.lead[step:]
        if step < 3:
            split_into(outs[2 * g], outs[2 * g + 1], lead, axis, mine, read)
        else:
            rows = slice(at, at + held.shape[-2])
            at = at + held.shape[-2]
            for to, where in halved(lead, axis, 1 - mine):
                outs[0][to + (rows,)] = read(where).astype(BF16)
            for to, where in halved(lead, axis, mine):
                outs[1][to + (rows,)] = read(where)


def single_kernel(plan, step, spot_ref, held, got, send, keep):
    split_into(
        send, keep, plan.lead[step:], plan.axis(0, step), bit_of(spot_ref, plan.orders[0][step]),
        lambda where: held[where] + got[where].astype(F32),
    )


def join_kernel(plan, spot_ref, held, got, held_other, got_other, conv_ref, down_ref, turned, down_turned):
    core = spot_ref[0] & 1
    group = plan.group
    rows, down_rows = plan.rows, plan.down_rows
    own = held[...] + got[...].astype(F32)
    other = held_other[...] + got_other[...].astype(F32)
    first, second = jnp.where(core == 0, own, other), jnp.where(core == 0, other, own)

    def merged(begin, end):
        pieces = []
        for at in range(begin, end, group):
            pieces += [first[at : at + group], second[at : at + group]]
        return pieces

    cut = plan.cuts[0][1]
    conv = merged(0, cut) + merged(cut + down_rows, rows + down_rows)
    down = merged(cut, cut + down_rows)
    width = own.shape[1] // 2
    for ref, pieces, space in ((conv_ref, conv, turned), (down_ref, down, down_turned)):
        space[...] = jnp.concatenate(pieces, axis=0).T
        ref[...] = space[pl.ds(pl.multiple_of(core * width, width), width)]


def input_kernel(plan, spot_ref, clip_ref, here_ref, here_other, side_ref, side_other, far_ref, far_other, next_ref,
                 down_ref, weight_ref, out_ref, done_ref, grads):
    cols, chans = plan.cols, plan.chans
    cells = clip_ref.shape[0]
    span = side_ref.shape[0]
    half = span // cols
    core = spot_ref[0] & 1
    side = 2 * (spot_ref[1] & 1)
    rows = ((here_ref, here_other), (side_ref, side_other), (far_ref, far_other))
    for slot, (own, other) in enumerate(rows):
        following = jnp.where(core == 0, other[...], next_ref[slot])
        every = jnp.concatenate([own[...], following], axis=0)
        here = every[: (half + 1) * cols]
        after = every[cols : (half + 2) * cols]
        even = (dot_nt(after, down_ref[0]) + dot_nt(here, down_ref[2])).astype(BF16)
        odd = dot_nt(after, down_ref[1]).astype(BF16)
        for u in range(half + 1):
            grads[slot, 2 * u * cols : (2 * u + 1) * cols] = even[u * cols : (u + 1) * cols]
            grads[slot, (2 * u + 1) * cols : (2 * u + 2) * cols] = odd[u * cols : (u + 1) * cols]
    acc = [jnp.zeros((cells, chans), F32) for _ in range(3)]
    for a in range(3):
        for slot, b in enumerate((1, side, 2 - side)):
            begin = (2 - a) * cols
            part = grads[slot, begin : begin + cells]
            for c in range(3):
                acc[c] = acc[c] + dot_nt(part, weight_ref[a * 3 + b, c * chans : (c + 1) * chans])
    grad_act = acc[1]
    for c in (0, 2):
        grad_act = grad_act + shifted_rows(acc[c], 1 - c, cols)
    value = clip_ref[...].astype(F32)
    sig = 1.0 / (1.0 + jnp.exp(-value))
    own = grads[0, :cells].astype(F32)
    out_ref[...] = (own + grad_act * (sig * (1.0 + value * (1.0 - sig)))).astype(BF16)
    done_ref[...] = jnp.zeros_like(done_ref)


def shape(dims, dtype):
    return jax.ShapeDtypeStruct(dims, dtype)


def call(kernel, scalars, args, outs, scratch=(), us=1, limit=48, after=(), left=0):
    vmem, smem = pl.BlockSpec(memory_space=pltpu.VMEM), pl.BlockSpec(memory_space=pltpu.SMEM)
    hbm = pl.BlockSpec(memory_space=pltpu.HBM)
    args = [pltpu.with_memory_space_constraint(a, pltpu.HBM) for a in args[:left]] + list(args[left:])
    after = list(after)
    size = sum(a.size * a.dtype.itemsize for a in args)
    given = len(scalars) + len(args)

    def run(*refs):
        kernel(*refs[:given], *refs[given + len(after) :])

    return pl.pallas_call(
        run,
        out_shape=outs,
        in_specs=[smem] * len(scalars) + [hbm] * left + [vmem] * (len(args) - left) + [vmem] * len(after),
        out_specs=jax.tree.map(lambda _: vmem, outs),
        scratch_shapes=list(scratch),
        compiler_params=pltpu.CompilerParams(vmem_limit_bytes=limit * MIB),
        cost_estimate=pl.CostEstimate(flops=int(us * 1.15e9), bytes_accessed=size, transcendentals=0),
    )(*scalars, *args, *after)


class Plan:
    def __init__(self, count, cols, chans):
        nbits = count.bit_length() - 1
        self.cols, self.chans = cols, chans
        self.rows, self.down_rows = 27 * chans // count // 2, 3 * chans // count // 2
        self.group = math.gcd(16, math.gcd(self.rows, self.down_rows))
        self.lead = (2,) * (1 + nbits)
        links = [(0, 1)] + [(1, i) for i in range(nbits)]
        self.place = {link: (0 if link[0] == 0 else nbits - link[1]) for link in links}
        tops, tail = links[:3], links[3:]
        self.orders = [tops[g:] + tops[:g] + tail for g in range(3)]
        third = (self.rows + self.down_rows) // 3
        cut = third - self.down_rows
        self.cuts = [(0, cut), (cut, cut + third), (cut + third, self.rows)]

    def spot(self, h):
        nbits = len(self.lead) - 1
        return tuple(h >> (nbits - 1 - i) & 1 for i in range(nbits))

    def axis(self, g, step):
        order = self.orders[g]
        return sum(self.place[link] < self.place[order[step]] for link in order[step + 1 :])


def swapped(value, link):
    axis = ("tm", "height")[link[0]]
    return lax.ppermute(value, axis, [(i, i ^ (1 << link[1])) for i in range(lax.axis_size(axis))])


def body(clip, conv_weight, down_weight, grad_out):
    nframes, nrows, ncols, chans = clip.shape
    half = grad_out.shape[0]
    cells, span = nframes * ncols, half * ncols
    tm_count, count = lax.axis_size("tm"), lax.axis_size("height")
    plan = Plan(count, ncols, chans)
    spot = jnp.stack([lax.axis_index("tm"), lax.axis_index("height")]).astype(jnp.int32)
    mine = grad_out.reshape(span, chans)
    flat = clip.reshape(cells, chans)
    weight = conv_weight.reshape(9, 3 * chans, chans)
    core_link = (0, 0)
    part = chans // 2
    wide = 3 * part
    lead = plan.lead
    pair = 2 * span

    side = swapped(mine, (1, 0))
    here_other = swapped(mine, core_link)
    clip_other = swapped(flat, core_link)
    first = lax.ppermute(flat, "tm", [(i, i + 1) for i in range(1, tm_count - 1, 2)])
    second = lax.ppermute(clip_other, "tm", [(i, i + 3) for i in range(0, tm_count - 3, 2)])
    listed = (9, 3, part // plan.group, 2, plan.group, chans)
    turned, spread = call(
        functools.partial(weights_kernel, plan), [spot], [weight.reshape(listed), down_weight],
        [shape((9, chans, wide), BF16), shape((2 * wide, chans), BF16)],
        [pltpu.VMEM(listed[:3] + listed[4:], BF16), pltpu.VMEM(down_weight.shape, BF16), pltpu.SemaphoreType.DMA((10,))],
        us=3, limit=16, left=2,
    )
    far = lax.ppermute(
        side, "height", [(i, i + (2 if i % 2 == 0 else -2)) for i in range(count) if 0 <= i + (2 if i % 2 == 0 else -2) < count]
    )
    side_other = swapped(side, core_link)

    terms = [shape((3, wide, chans), F32), shape((chans, 3 * chans), F32)]
    even, odd, own_conv, own_sum, plus = call(
        functools.partial(own_kernel, plan), [spot],
        [flat, clip_other, first, second, mine, here_other, spread, turned],
        [shape((wide, 3 * cells // 2), BF16), shape((wide, 3 * cells // 2), BF16), *terms, shape((part, 3 * chans), F32)],
        [pltpu.VMEM((3 * cells, chans), BF16), pltpu.VMEM((pair, chans), BF16)], us=3, limit=20,
    )
    far, plus = lax.optimization_barrier((far, plus))
    far_other = swapped(far, core_link)
    side_conv, side_sum = call(
        functools.partial(side_kernel, plan), [spot], [side, side_other, even, odd, spread, turned], terms,
        [pltpu.VMEM((pair, chans), BF16)], us=2, limit=20,
    )
    outs = [shape((3, span, chans), BF16)]
    for begin, end in plan.cuts:
        outs += [shape(lead[1:] + (end - begin, part), BF16), shape(lead[1:] + (end - begin, part), F32)]
    down_dims = lead + (plan.down_rows, part)
    outs += [shape(down_dims, BF16), shape(down_dims, F32)]
    result = call(
        functools.partial(far_kernel, plan), [spot],
        [mine, side, far, far_other, even, odd, own_conv, own_sum, plus, side_conv, side_sum, spread, turned], outs,
        [pltpu.VMEM((pair, chans), BF16), pltpu.VMEM((3, wide, chans), F32), pltpu.VMEM(lead + (plan.rows, part), F32)],
        us=3, limit=20,
    )
    head = result[0]
    held = []
    for g in range(3):
        held += [result[2 + 2 * g], swapped(result[1 + 2 * g], plan.orders[g][0])]
    send, keep = call(
        functools.partial(single_kernel, plan, 0), [spot], [result[8], swapped(result[7], core_link)],
        [shape(down_dims[1:], BF16), shape(down_dims[1:], F32)], limit=8,
    )
    down_held = [keep, swapped(send, plan.orders[0][0])]
    following = lax.ppermute(head, "tm", [(i + 1, i) for i in range(1, tm_count - 1, 2)])
    grad_input, done = call(
        functools.partial(input_kernel, plan), [spot],
        [flat, mine, here_other, side, side_other, far, far_other, following, down_weight, weight],
        [shape((cells, chans), BF16), shape((8, part), F32)],
        [pltpu.VMEM((3, (2 * half + 2) * ncols, chans), BF16)],
        us=4, limit=24,
    )
    for step in (1, 2):
        outs = []
        for g in range(3):
            rows = plan.cuts[g][1] - plan.cuts[g][0] + (plan.down_rows if g == 0 else 0)
            outs += [shape(lead[step + 1 :] + (rows, part), BF16), shape(lead[step + 1 :] + (rows, part), F32)]
        extra = down_held if step == 1 else []
        result = call(functools.partial(fold_kernel, plan, step), [spot], held + extra, outs, limit=12)
        held = []
        for g in range(3):
            held += [result[2 * g + 1], swapped(result[2 * g], plan.orders[g][step])]
    for step in range(3, len(lead)):
        dims = lead[step + 1 :] + (plan.rows + plan.down_rows, part)
        kernel = fold_kernel if step == 3 else single_kernel
        send, keep = call(
            functools.partial(kernel, plan, step), [spot], held, [shape(dims, BF16), shape(dims, F32)], limit=8,
            after=[done] if step == 3 else (),
        )
        held = [keep, swapped(send, plan.orders[0][step])]
    grad_conv, grad_down = call(
        functools.partial(join_kernel, plan), [spot], held + [swapped(v, core_link) for v in held],
        [shape((part // 2, 2 * plan.rows), F32), shape((part // 2, 2 * plan.down_rows), F32)],
        [pltpu.VMEM((part, 2 * plan.rows), F32), pltpu.VMEM((part, 2 * plan.down_rows), F32)],
        limit=8,
    )
    return (grad_input.reshape(clip.shape), grad_conv.T, grad_down.T)


def solution(mesh):
    placed = (P("tm", "height", None, None), P(), P(), P("tm", "height", None, None))
    return jax.shard_map(
        body,
        mesh=mesh,
        in_specs=placed,
        out_specs=(P("tm", "height", None, None), P("height", "tm"), P("height", "tm")),
        check_vma=False,
    )
```

```python
import functools
import math

import jax
import jax.numpy as jnp
from jax import lax
from jax.experimental import pallas as pl
from jax.experimental.pallas import tpu as pltpu
from jax.sharding import PartitionSpec as P

F32 = jnp.float32
BF16 = jnp.bfloat16
MIB = 1024 * 1024


def dot(left, right):
    return jnp.dot(left, right, preferred_element_type=F32)


def dot_nt(left, right):
    return lax.dot_general(left, right, (((1,), (1,)), ((), ())), preferred_element_type=F32)


def shifted_rows(value, step, period):
    if step == 0:
        return value
    rows = value.shape[0]
    moved = pltpu.roll(value, (-step) % rows, 0)
    place = lax.broadcasted_iota(jnp.int32, value.shape, 0) % period + step
    return jnp.where(jnp.logical_and(place >= 0, place < period), moved, 0.0)


def channel_of(place, group, core):
    return (place // group * 2 + core) * group + place % group


def one_hot(wanted, chans):
    dims = (wanted.shape[0], chans)
    return (lax.broadcasted_iota(jnp.int32, dims, 1) == wanted).astype(F32).astype(BF16)


def picker(chans, group, core):
    place = lax.broadcasted_iota(jnp.int32, (chans // 2, chans), 0)
    return one_hot(channel_of(place, group, core), chans)


def lay_pair(window, core, own, other, begin=0):
    size = own.shape[0]
    window[pl.ds(pl.multiple_of(begin + size * core, size), size)] = own[...]
    window[pl.ds(pl.multiple_of(begin + size * (1 - core), size), size)] = other[...]


def silu(value):
    return value / (1.0 + jnp.exp(-value))


def halved(lead, axis, index):
    rest = lead[:axis] + lead[axis + 1 :]
    for flat in range(math.prod(rest)):
        spot, left = [], flat
        for extent in reversed(rest):
            spot.insert(0, left % extent)
            left //= extent
        yield tuple(spot), tuple(spot[:axis]) + (index,) + tuple(spot[axis:])


def bit_of(spot_ref, link):
    return lax.shift_right_logical(spot_ref[link[0]], link[1]) & 1


def split_into(send, keep, lead, axis, mine, read):
    for to, where in halved(lead, axis, 1 - mine):
        send[to] = read(where).astype(send.dtype)
    for to, where in halved(lead, axis, mine):
        keep[to] = read(where)


def weights_kernel(plan, spot_ref, weight_ref, down_ref, turned_ref, spread_ref, weights, downs, sems):
    chans = plan.chans
    core = spot_ref[0] & 1
    copies = [pltpu.make_async_copy(down_ref, downs, sems.at[9])]
    copies += [pltpu.make_async_copy(weight_ref.at[ab, :, :, core], weights.at[ab], sems.at[ab]) for ab in range(9)]
    for copy in copies:
        copy.start()
    copies[0].wait()
    for k in range(3):
        spread_ref[k * chans : (k + 1) * chans] = downs[k].T
    for ab in range(9):
        copies[ab + 1].wait()
        block = weights[ab].reshape(3 * chans // 2, chans)
        turned_ref[ab] = block.T


def row_terms(plan, even, odd, cells, spread_ref, turned_ref, b, conv_ref):
    chans = plan.chans
    span = cells.shape[0]
    cross = []
    for s in range(5):
        begin = s // 2 * plan.cols
        cross.append(dot((even, odd)[s % 2][:, begin : begin + span], cells).astype(BF16))
    threes = [jnp.concatenate(cross[a : a + 3], axis=1) for a in range(3)]
    for a in range(3):
        conv_ref[a] = dot(threes[a], spread_ref[...])
    turned = jnp.concatenate([turned_ref[a * 3 + b] for a in range(3)], axis=1)
    down = dot(turned, jnp.concatenate(threes, axis=0))
    return down


def own_kernel(plan, spot_ref, clip_ref, clip_other, first_ref, second_ref, here_ref, here_other, spread_ref, turned_ref,
               even_ref, odd_ref, conv_ref, sum_ref, plus_ref, clips, cells):
    cols, chans = plan.cols, plan.chans
    part = chans // 2
    core = spot_ref[0] & 1
    rows = clip_ref.shape[0]
    clips[:rows] = first_ref[...] + second_ref[...]
    lay_pair(clips, core, clip_ref, clip_other, rows)
    lay_pair(cells, core, here_ref, here_other)
    pick = picker(chans, plan.group, core)
    plain = dot_nt(pick, clips[...])
    chosen = silu(plain).astype(BF16).astype(F32)
    plain = plain.astype(BF16)
    steps = lax.broadcasted_iota(jnp.int32, chosen.shape, 1) % cols
    count = 3 * rows // cols // 2
    for c in range(3):
        moved = chosen
        if c != 1:
            moved = pltpu.roll(chosen, (1 - c) % chosen.shape[1], 1)
            moved = jnp.where(steps == (0 if c == 0 else cols - 1), 0.0, moved)
        moved = moved.astype(BF16)
        lanes = slice(c * part, (c + 1) * part)
        for f in range(count):
            to = slice(f * cols, (f + 1) * cols)
            even_ref[lanes, to] = moved[:, 2 * f * cols : (2 * f + 1) * cols]
            odd_ref[lanes, to] = moved[:, (2 * f + 1) * cols : (2 * f + 2) * cols]
    here = cells[...]
    for k in range(3):
        halves = [plain[:, (2 * f + k % 2) * cols : (2 * f + k % 2 + 1) * cols] for f in range(count)]
        begin = 1 + k // 2
        frames = jnp.concatenate(halves[begin : begin + here.shape[0] // cols], axis=1)
        plus_ref[:, k * chans : (k + 1) * chans] = dot(frames, here)
    sum_ref[...] = row_terms(plan, even_ref, odd_ref, here, spread_ref, turned_ref, 1, conv_ref)


def side_kernel(plan, spot_ref, side_ref, side_other, even_ref, odd_ref, spread_ref, turned_ref, conv_ref, sum_ref, cells):
    lay_pair(cells, spot_ref[0] & 1, side_ref, side_other)
    b = 2 * (spot_ref[1] & 1)
    sum_ref[...] = row_terms(plan, even_ref, odd_ref, cells[...], spread_ref, turned_ref, b, conv_ref)


def far_kernel(plan, spot_ref, here_ref, side_ref, far_ref, far_other, even_ref, odd_ref, own_conv, own_sum, plus_ref, side_conv,
               side_sum, spread_ref, turned_ref, head_ref, *rest):
    outs, (cells, conv, total) = rest[:-3], rest[-3:]
    chans = plan.chans
    part = chans // 2
    core = spot_ref[0] & 1
    odd_row = spot_ref[1] & 1
    lay_pair(cells, core, far_ref, far_other)
    down = row_terms(plan, even_ref, odd_ref, cells[...], spread_ref, turned_ref, 2 - 2 * odd_row, conv)
    down = own_sum[...] + side_sum[...] + down
    for slot, ref in enumerate((here_ref, side_ref, far_ref)):
        head_ref[slot] = ref[...]
    wide = 3 * part

    def place(a, b, value):
        first = (a * 3 + b) * wide
        begin = first
        while begin < first + wide:
            h = begin // plan.rows
            end = min((h + 1) * plan.rows, first + wide)
            for y in range(2):
                total[(y,) + plan.spot(h) + (slice(begin - h * plan.rows, end - h * plan.rows),)] = value[
                    begin - first : end - first, y * part : (y + 1) * part
                ]
            begin = end

    for a in range(3):
        place(a, 1, own_conv[a])
    for parity in range(2):
        @pl.when(odd_row == parity)
        def _():
            for a in range(3):
                place(a, 2 * parity, side_conv[a])
                place(a, 2 - 2 * parity, conv[a])
    for g in range(3):
        link = plan.orders[g][0]
        begin, end = plan.cuts[g]
        split_into(
            outs[2 * g], outs[2 * g + 1], plan.lead, plan.axis(g, 0), bit_of(spot_ref, link),
            lambda where: total[where + (slice(begin, end),)],
        )
    mine = core == 0
    pairs = range(0, chans, 2 * plan.group)
    low = jnp.concatenate([down[i : i + plan.group] for i in pairs], axis=0)
    high = jnp.concatenate([down[i + plan.group : i + 2 * plan.group] for i in pairs], axis=0)
    keep = jnp.where(mine, low, high) + plus_ref[...]
    for ref, value in ((outs[6], jnp.where(mine, high, low)), (outs[7], keep)):
        for h in range(math.prod(plan.lead[1:])):
            begin = h * plan.down_rows
            while begin < (h + 1) * plan.down_rows:
                k = begin // part
                end = min((k + 1) * part, (h + 1) * plan.down_rows)
                for y in range(2):
                    ref[(y,) + plan.spot(h) + (slice(begin - h * plan.down_rows, end - h * plan.down_rows),)] = value[
                        begin - k * part : end - k * part, k * chans + y * part : k * chans + (y + 1) * part
                    ].astype(ref.dtype)
                begin = end


def merge_kernel(plan, step, spot_ref, *refs):
    ins, (send, keep) = refs[:-2], refs[-2:]

    def read(where):
        return jnp.concatenate([ins[i][where] + ins[i + 1][where].astype(F32) for i in range(0, len(ins), 2)], axis=0)

    split_into(send, keep, plan.lead[step:], plan.axis(0, step), bit_of(spot_ref, plan.orders[0][step]), read)


def single_kernel(plan, g, step, spot_ref, *refs):
    ins, (send, keep) = refs[:-2], refs[-2:]

    def read(where):
        pieces = [ins[i][where] + ins[i + 1][where].astype(F32) for i in range(0, len(ins), 2)]
        return pieces[0] if len(pieces) == 1 else jnp.concatenate(pieces, axis=0)

    split_into(send, keep, plan.lead[step:], plan.axis(g, step), bit_of(spot_ref, plan.orders[g][step]), read)


def join_kernel(plan, spot_ref, held, got, held_other, got_other, conv_ref, down_ref, turned, down_turned):
    core = spot_ref[0] & 1
    group = plan.group
    rows, down_rows = plan.rows, plan.down_rows
    own = held[...] + got[...].astype(F32)
    other = held_other[...] + got_other[...].astype(F32)
    first, second = jnp.where(core == 0, own, other), jnp.where(core == 0, other, own)

    def merged(begin, end):
        pieces = []
        for at in range(begin, end, group):
            pieces += [first[at : at + group], second[at : at + group]]
        return pieces

    cut = plan.cuts[0][1]
    conv = merged(0, cut) + merged(cut + down_rows, rows + down_rows)
    down = merged(cut, cut + down_rows)
    width = own.shape[1] // 2
    for ref, pieces, space in ((conv_ref, conv, turned), (down_ref, down, down_turned)):
        space[...] = jnp.concatenate(pieces, axis=0).T
        ref[...] = space[pl.ds(pl.multiple_of(core * width, width), width)]


def input_kernel(plan, spot_ref, clip_ref, here_ref, here_other, side_ref, side_other, far_ref, far_other, next_ref,
                 down_ref, weight_ref, out_ref, done_ref, grads):
    cols, chans = plan.cols, plan.chans
    cells = clip_ref.shape[0]
    span = side_ref.shape[0]
    half = span // cols
    core = spot_ref[0] & 1
    side = 2 * (spot_ref[1] & 1)
    rows = ((here_ref, here_other), (side_ref, side_other), (far_ref, far_other))
    for slot, (own, other) in enumerate(rows):
        following = jnp.where(core == 0, other[...], next_ref[slot])
        every = jnp.concatenate([own[...], following], axis=0)
        here = every[: (half + 1) * cols]
        after = every[cols : (half + 2) * cols]
        even = (dot_nt(after, down_ref[0]) + dot_nt(here, down_ref[2])).astype(BF16)
        odd = dot_nt(after, down_ref[1]).astype(BF16)
        for u in range(half + 1):
            grads[slot, 2 * u * cols : (2 * u + 1) * cols] = even[u * cols : (u + 1) * cols]
            grads[slot, (2 * u + 1) * cols : (2 * u + 2) * cols] = odd[u * cols : (u + 1) * cols]
    taps = [(a, slot, b) for a in range(3) for slot, b in enumerate((1, side, 2 - side))]
    left = jnp.concatenate([grads[slot, (2 - a) * cols : (2 - a) * cols + cells] for a, slot, _ in taps], axis=1)
    acc = []
    for c in range(3):
        right = jnp.concatenate([weight_ref[a * 3 + b, c * chans : (c + 1) * chans] for a, _, b in taps], axis=1)
        acc.append(dot_nt(left, right))
    grad_act = acc[1]
    for c in (0, 2):
        grad_act = grad_act + shifted_rows(acc[c], 1 - c, cols)
    value = clip_ref[...].astype(F32)
    sig = 1.0 / (1.0 + jnp.exp(-value))
    own = grads[0, :cells].astype(F32)
    out_ref[...] = (own + grad_act * (sig * (1.0 + value * (1.0 - sig)))).astype(BF16)
    done_ref[...] = jnp.zeros_like(done_ref)


def shape(dims, dtype):
    return jax.ShapeDtypeStruct(dims, dtype)


def call(kernel, scalars, args, outs, scratch=(), us=1, limit=48, after=(), left=0):
    vmem, smem = pl.BlockSpec(memory_space=pltpu.VMEM), pl.BlockSpec(memory_space=pltpu.SMEM)
    hbm = pl.BlockSpec(memory_space=pltpu.HBM)
    args = [pltpu.with_memory_space_constraint(a, pltpu.HBM) for a in args[:left]] + list(args[left:])
    after = list(after)
    size = sum(a.size * a.dtype.itemsize for a in args)
    given = len(scalars) + len(args)

    def run(*refs):
        kernel(*refs[:given], *refs[given + len(after) :])

    return pl.pallas_call(
        run,
        out_shape=outs,
        in_specs=[smem] * len(scalars) + [hbm] * left + [vmem] * (len(args) - left) + [vmem] * len(after),
        out_specs=jax.tree.map(lambda _: vmem, outs),
        scratch_shapes=list(scratch),
        compiler_params=pltpu.CompilerParams(vmem_limit_bytes=limit * MIB),
        cost_estimate=pl.CostEstimate(flops=int(us * 1.15e9), bytes_accessed=size, transcendentals=0),
    )(*scalars, *args, *after)


class Plan:
    def __init__(self, count, cols, chans):
        nbits = count.bit_length() - 1
        self.cols, self.chans = cols, chans
        self.rows, self.down_rows = 27 * chans // count // 2, 3 * chans // count // 2
        self.group = math.gcd(16, math.gcd(self.rows, self.down_rows))
        self.lead = (2,) * (1 + nbits)
        links = [(0, 1)] + [(1, i) for i in range(nbits)]
        self.place = {link: (0 if link[0] == 0 else nbits - link[1]) for link in links}
        tops, tail = links[:3], links[3:]
        self.orders = [tops[g:] + tops[:g] + tail for g in range(3)]
        third = (self.rows + self.down_rows) // 3
        cut = third - self.down_rows
        self.cuts = [(0, cut), (cut, cut + third), (cut + third, self.rows)]

    def spot(self, h):
        nbits = len(self.lead) - 1
        return tuple(h >> (nbits - 1 - i) & 1 for i in range(nbits))

    def axis(self, g, step):
        order = self.orders[g]
        return sum(self.place[link] < self.place[order[step]] for link in order[step + 1 :])


def swapped(value, link):
    axis = ("tm", "height")[link[0]]
    return lax.ppermute(value, axis, [(i, i ^ (1 << link[1])) for i in range(lax.axis_size(axis))])


def body(clip, conv_weight, down_weight, grad_out):
    nframes, nrows, ncols, chans = clip.shape
    half = grad_out.shape[0]
    cells, span = nframes * ncols, half * ncols
    tm_count, count = lax.axis_size("tm"), lax.axis_size("height")
    plan = Plan(count, ncols, chans)
    spot = jnp.stack([lax.axis_index("tm"), lax.axis_index("height")]).astype(jnp.int32)
    mine = grad_out.reshape(span, chans)
    flat = clip.reshape(cells, chans)
    weight = conv_weight.reshape(9, 3 * chans, chans)
    core_link = (0, 0)
    part = chans // 2
    wide = 3 * part
    lead = plan.lead
    pair = 2 * span

    side = swapped(mine, (1, 0))
    here_other = swapped(mine, core_link)
    clip_other = swapped(flat, core_link)
    first = lax.ppermute(flat, "tm", [(i, i + 1) for i in range(1, tm_count - 1, 2)])
    second = lax.ppermute(clip_other, "tm", [(i, i + 3) for i in range(0, tm_count - 3, 2)])
    listed = (9, 3, part // plan.group, 2, plan.group, chans)
    turned, spread = call(
        functools.partial(weights_kernel, plan), [spot], [weight.reshape(listed), down_weight],
        [shape((9, chans, wide), BF16), shape((2 * wide, chans), BF16)],
        [pltpu.VMEM(listed[:3] + listed[4:], BF16), pltpu.VMEM(down_weight.shape, BF16), pltpu.SemaphoreType.DMA((10,))],
        us=3, limit=16, left=2,
    )
    far = lax.ppermute(
        side, "height", [(i, i + (2 if i % 2 == 0 else -2)) for i in range(count) if 0 <= i + (2 if i % 2 == 0 else -2) < count]
    )
    side_other = swapped(side, core_link)

    terms = [shape((3, wide, chans), F32), shape((chans, 3 * chans), F32)]
    even, odd, own_conv, own_sum, plus = call(
        functools.partial(own_kernel, plan), [spot],
        [flat, clip_other, first, second, mine, here_other, spread, turned],
        [shape((wide, 3 * cells // 2), BF16), shape((wide, 3 * cells // 2), BF16), *terms, shape((part, 3 * chans), F32)],
        [pltpu.VMEM((3 * cells, chans), BF16), pltpu.VMEM((pair, chans), BF16)], us=3, limit=20,
    )
    far, plus = lax.optimization_barrier((far, plus))
    far_other = swapped(far, core_link)
    side_conv, side_sum = call(
        functools.partial(side_kernel, plan), [spot], [side, side_other, even, odd, spread, turned], terms,
        [pltpu.VMEM((pair, chans), BF16)], us=2, limit=20,
    )
    outs = [shape((3, span, chans), BF16)]
    for begin, end in plan.cuts:
        outs += [shape(lead[1:] + (end - begin, part), BF16), shape(lead[1:] + (end - begin, part), F32)]
    down_dims = lead + (plan.down_rows, part)
    outs += [shape(down_dims, BF16), shape(down_dims, F32)]
    result = call(
        functools.partial(far_kernel, plan), [spot],
        [mine, side, far, far_other, even, odd, own_conv, own_sum, plus, side_conv, side_sum, spread, turned], outs,
        [pltpu.VMEM((pair, chans), BF16), pltpu.VMEM((3, wide, chans), F32), pltpu.VMEM(lead + (plan.rows, part), F32)],
        us=3, limit=20,
    )
    head = result[0]
    held = []
    for g in range(3):
        held += [result[2 + 2 * g], swapped(result[1 + 2 * g], plan.orders[g][0])]
    send, keep = call(
        functools.partial(single_kernel, plan, 0, 0), [spot], [result[8], swapped(result[7], core_link)],
        [shape(down_dims[1:], BF16), shape(down_dims[1:], F32)], limit=8,
    )
    down_held = [keep, swapped(send, plan.orders[0][0])]
    following = lax.ppermute(head, "tm", [(i + 1, i) for i in range(1, tm_count - 1, 2)])
    grad_input, done = call(
        functools.partial(input_kernel, plan), [spot],
        [flat, mine, here_other, side, side_other, far, far_other, following, down_weight, weight],
        [shape((cells, chans), BF16), shape((8, part), F32)],
        [pltpu.VMEM((3, (2 * half + 2) * ncols, chans), BF16)],
        us=4, limit=24,
    )
    held = [held[:2] + down_held, held[2:4], held[4:6]]
    for step in (1, 2):
        for g in range(3):
            rows = plan.cuts[g][1] - plan.cuts[g][0] + (plan.down_rows if g == 0 else 0)
            dims = lead[step + 1 :] + (rows, part)
            send, keep = call(
                functools.partial(single_kernel, plan, g, step), [spot], held[g], [shape(dims, BF16), shape(dims, F32)],
                us=0.5, limit=8,
            )
            held[g] = [keep, swapped(send, plan.orders[g][step])]
    held = sum(held, [])
    for step in range(3, len(lead)):
        dims = lead[step + 1 :] + (plan.rows + plan.down_rows, part)
        send, keep = call(
            functools.partial(merge_kernel, plan, step), [spot], held, [shape(dims, BF16), shape(dims, F32)], limit=8,
            after=[done] if step == 3 else (),
        )
        held = [keep, swapped(send, plan.orders[0][step])]
    grad_conv, grad_down = call(
        functools.partial(join_kernel, plan), [spot], held + [swapped(v, core_link) for v in held],
        [shape((part // 2, 2 * plan.rows), F32), shape((part // 2, 2 * plan.down_rows), F32)],
        [pltpu.VMEM((part, 2 * plan.rows), F32), pltpu.VMEM((part, 2 * plan.down_rows), F32)],
        limit=8,
    )
    return (grad_input.reshape(clip.shape), grad_conv.T, grad_down.T)


def solution(mesh):
    placed = (P("tm", "height", None, None), P(), P(), P("tm", "height", None, None))
    return jax.shard_map(
        body,
        mesh=mesh,
        in_specs=placed,
        out_specs=(P("tm", "height", None, None), P("height", "tm"), P("height", "tm")),
        check_vma=False,
    )
```

```python
import functools
import math

import jax
import jax.numpy as jnp
from jax import lax
from jax.experimental import pallas as pl
from jax.experimental.pallas import tpu as pltpu
from jax.sharding import PartitionSpec as P

F32 = jnp.float32
BF16 = jnp.bfloat16
MIB = 1024 * 1024


def dot(left, right):
    return jnp.dot(left, right, preferred_element_type=F32)


def dot_nt(left, right):
    return lax.dot_general(left, right, (((1,), (1,)), ((), ())), preferred_element_type=F32)


def shifted_rows(value, step, period):
    if step == 0:
        return value
    rows = value.shape[0]
    moved = pltpu.roll(value, (-step) % rows, 0)
    place = lax.broadcasted_iota(jnp.int32, value.shape, 0) % period + step
    return jnp.where(jnp.logical_and(place >= 0, place < period), moved, 0.0)


def channel_of(place, group, core):
    return (place // group * 2 + core) * group + place % group


def one_hot(wanted, chans):
    dims = (wanted.shape[0], chans)
    return (lax.broadcasted_iota(jnp.int32, dims, 1) == wanted).astype(F32).astype(BF16)


def picker(chans, group, core):
    place = lax.broadcasted_iota(jnp.int32, (chans // 2, chans), 0)
    return one_hot(channel_of(place, group, core), chans)


def lay_pair(window, core, own, other, begin=0):
    size = own.shape[0]
    window[pl.ds(pl.multiple_of(begin + size * core, size), size)] = own[...]
    window[pl.ds(pl.multiple_of(begin + size * (1 - core), size), size)] = other[...]


def silu(value):
    return value / (1.0 + jnp.exp(-value))


def halved(lead, axis, index):
    rest = lead[:axis] + lead[axis + 1 :]
    for flat in range(math.prod(rest)):
        spot, left = [], flat
        for extent in reversed(rest):
            spot.insert(0, left % extent)
            left //= extent
        yield tuple(spot), tuple(spot[:axis]) + (index,) + tuple(spot[axis:])


def bit_of(spot_ref, link):
    return lax.shift_right_logical(spot_ref[link[0]], link[1]) & 1


def split_into(send, keep, lead, axis, mine, read):
    for to, where in halved(lead, axis, 1 - mine):
        send[to] = read(where).astype(send.dtype)
    for to, where in halved(lead, axis, mine):
        keep[to] = read(where)


def weights_kernel(plan, spot_ref, weight_ref, down_ref, turned_ref, spread_ref, weights, downs, sems):
    chans = plan.chans
    core = spot_ref[0] & 1
    copies = [pltpu.make_async_copy(down_ref, downs, sems.at[9])]
    copies += [pltpu.make_async_copy(weight_ref.at[ab, :, :, core], weights.at[ab], sems.at[ab]) for ab in range(9)]
    for copy in copies:
        copy.start()
    copies[0].wait()
    for k in range(3):
        spread_ref[k * chans : (k + 1) * chans] = downs[k].T
    for ab in range(9):
        copies[ab + 1].wait()
        block = weights[ab].reshape(3 * chans // 2, chans)
        turned_ref[ab] = block.T


def row_terms(plan, even, odd, cells, spread_ref, turned_ref, b, conv_ref):
    chans = plan.chans
    span = cells.shape[0]
    cross = []
    for s in range(5):
        begin = s // 2 * plan.cols
        cross.append(dot((even, odd)[s % 2][:, begin : begin + span], cells).astype(BF16))
    threes = [jnp.concatenate(cross[a : a + 3], axis=1) for a in range(3)]
    for a in range(3):
        conv_ref[a] = dot(threes[a], spread_ref[...])
    turned = jnp.concatenate([turned_ref[a * 3 + b] for a in range(3)], axis=1)
    down = dot(turned, jnp.concatenate(threes, axis=0))
    return down


def own_kernel(plan, spot_ref, clip_ref, clip_other, first_ref, second_ref, here_ref, here_other, spread_ref, turned_ref,
               even_ref, odd_ref, conv_ref, sum_ref, plus_ref, clips, cells):
    cols, chans = plan.cols, plan.chans
    part = chans // 2
    core = spot_ref[0] & 1
    rows = clip_ref.shape[0]
    clips[:rows] = first_ref[...] + second_ref[...]
    lay_pair(clips, core, clip_ref, clip_other, rows)
    lay_pair(cells, core, here_ref, here_other)
    pick = picker(chans, plan.group, core)
    plain = dot_nt(pick, clips[...])
    chosen = silu(plain).astype(BF16).astype(F32)
    plain = plain.astype(BF16)
    steps = lax.broadcasted_iota(jnp.int32, chosen.shape, 1) % cols
    count = 3 * rows // cols // 2
    for c in range(3):
        moved = chosen
        if c != 1:
            moved = pltpu.roll(chosen, (1 - c) % chosen.shape[1], 1)
            moved = jnp.where(steps == (0 if c == 0 else cols - 1), 0.0, moved)
        moved = moved.astype(BF16)
        lanes = slice(c * part, (c + 1) * part)
        for f in range(count):
            to = slice(f * cols, (f + 1) * cols)
            even_ref[lanes, to] = moved[:, 2 * f * cols : (2 * f + 1) * cols]
            odd_ref[lanes, to] = moved[:, (2 * f + 1) * cols : (2 * f + 2) * cols]
    here = cells[...]
    for k in range(3):
        halves = [plain[:, (2 * f + k % 2) * cols : (2 * f + k % 2 + 1) * cols] for f in range(count)]
        begin = 1 + k // 2
        frames = jnp.concatenate(halves[begin : begin + here.shape[0] // cols], axis=1)
        plus_ref[:, k * chans : (k + 1) * chans] = dot(frames, here)
    sum_ref[...] = row_terms(plan, even_ref, odd_ref, here, spread_ref, turned_ref, 1, conv_ref)


def side_kernel(plan, spot_ref, side_ref, side_other, even_ref, odd_ref, spread_ref, turned_ref, conv_ref, sum_ref, cells):
    lay_pair(cells, spot_ref[0] & 1, side_ref, side_other)
    b = 2 * (spot_ref[1] & 1)
    sum_ref[...] = row_terms(plan, even_ref, odd_ref, cells[...], spread_ref, turned_ref, b, conv_ref)


def far_kernel(plan, spot_ref, here_ref, side_ref, far_ref, far_other, even_ref, odd_ref, own_conv, own_sum, plus_ref, side_conv,
               side_sum, spread_ref, turned_ref, head_ref, *rest):
    outs, (cells, conv, total) = rest[:-3], rest[-3:]
    chans = plan.chans
    part = chans // 2
    core = spot_ref[0] & 1
    odd_row = spot_ref[1] & 1
    lay_pair(cells, core, far_ref, far_other)
    down = row_terms(plan, even_ref, odd_ref, cells[...], spread_ref, turned_ref, 2 - 2 * odd_row, conv)
    down = own_sum[...] + side_sum[...] + down
    for slot, ref in enumerate((here_ref, side_ref, far_ref)):
        head_ref[slot] = ref[...]
    wide = 3 * part

    def place(a, b, value):
        first = (a * 3 + b) * wide
        begin = first
        while begin < first + wide:
            h = begin // plan.rows
            end = min((h + 1) * plan.rows, first + wide)
            for y in range(2):
                total[(y,) + plan.spot(h) + (slice(begin - h * plan.rows, end - h * plan.rows),)] = value[
                    begin - first : end - first, y * part : (y + 1) * part
                ]
            begin = end

    for a in range(3):
        place(a, 1, own_conv[a])
    for parity in range(2):
        @pl.when(odd_row == parity)
        def _():
            for a in range(3):
                place(a, 2 * parity, side_conv[a])
                place(a, 2 - 2 * parity, conv[a])
    for g in range(3):
        link = plan.orders[g][0]
        begin, end = plan.cuts[g]
        split_into(
            outs[2 * g], outs[2 * g + 1], plan.lead, plan.axis(g, 0), bit_of(spot_ref, link),
            lambda where: total[where + (slice(begin, end),)],
        )
    mine = core == 0
    pairs = range(0, chans, 2 * plan.group)
    low = jnp.concatenate([down[i : i + plan.group] for i in pairs], axis=0)
    high = jnp.concatenate([down[i + plan.group : i + 2 * plan.group] for i in pairs], axis=0)
    keep = jnp.where(mine, low, high) + plus_ref[...]
    for ref, value in ((outs[6], jnp.where(mine, high, low)), (outs[7], keep)):
        for h in range(math.prod(plan.lead[1:])):
            begin = h * plan.down_rows
            while begin < (h + 1) * plan.down_rows:
                k = begin // part
                end = min((k + 1) * part, (h + 1) * plan.down_rows)
                for y in range(2):
                    ref[(y,) + plan.spot(h) + (slice(begin - h * plan.down_rows, end - h * plan.down_rows),)] = value[
                        begin - k * part : end - k * part, k * chans + y * part : k * chans + (y + 1) * part
                    ].astype(ref.dtype)
                begin = end


def merge_kernel(plan, step, spot_ref, *refs):
    ins, (send, keep) = refs[:-2], refs[-2:]

    def read(where):
        return jnp.concatenate([ins[i][where] + ins[i + 1][where].astype(F32) for i in range(0, len(ins), 2)], axis=0)

    split_into(send, keep, plan.lead[step:], plan.axis(0, step), bit_of(spot_ref, plan.orders[0][step]), read)


def single_kernel(plan, g, step, spot_ref, *refs):
    ins, (send, keep) = refs[:-2], refs[-2:]

    def read(where):
        pieces = [ins[i][where] + ins[i + 1][where].astype(F32) for i in range(0, len(ins), 2)]
        return pieces[0] if len(pieces) == 1 else jnp.concatenate(pieces, axis=0)

    split_into(send, keep, plan.lead[step:], plan.axis(g, step), bit_of(spot_ref, plan.orders[g][step]), read)


def join_kernel(plan, spot_ref, held, got, held_other, got_other, conv_ref, down_ref, turned, down_turned):
    core = spot_ref[0] & 1
    group = plan.group
    rows, down_rows = plan.rows, plan.down_rows
    own = held[...] + got[...].astype(F32)
    other = held_other[...] + got_other[...].astype(F32)
    first, second = jnp.where(core == 0, own, other), jnp.where(core == 0, other, own)

    def merged(begin, end):
        pieces = []
        for at in range(begin, end, group):
            pieces += [first[at : at + group], second[at : at + group]]
        return pieces

    cut = plan.cuts[0][1]
    conv = merged(0, cut) + merged(cut + down_rows, rows + down_rows)
    down = merged(cut, cut + down_rows)
    width = own.shape[1] // 2
    for ref, pieces, space in ((conv_ref, conv, turned), (down_ref, down, down_turned)):
        space[...] = jnp.concatenate(pieces, axis=0).T
        ref[...] = space[pl.ds(pl.multiple_of(core * width, width), width)]


def grads_kernel(plan, spot_ref, here_ref, here_other, side_ref, side_other, far_ref, far_other, next_ref, spread_ref, grads, done_ref):
    cols, chans = plan.cols, plan.chans
    half = side_ref.shape[0] // cols
    core = spot_ref[0] & 1
    rows = ((here_ref, here_other), (side_ref, side_other), (far_ref, far_other))
    for slot, (own, other) in enumerate(rows):
        following = jnp.where(core == 0, other[...], next_ref[slot])
        every = jnp.concatenate([own[...], following], axis=0)
        here = every[: (half + 1) * cols]
        after = every[cols : (half + 2) * cols]
        even = (dot(after, spread_ref[:chans]) + dot(here, spread_ref[2 * chans :])).astype(BF16)
        odd = dot(after, spread_ref[chans : 2 * chans]).astype(BF16)
        for u in range(half + 1):
            grads[slot, 2 * u * cols : (2 * u + 1) * cols] = even[u * cols : (u + 1) * cols]
            grads[slot, (2 * u + 1) * cols : (2 * u + 2) * cols] = odd[u * cols : (u + 1) * cols]
    done_ref[...] = jnp.zeros_like(done_ref)


def input_kernel(plan, spot_ref, clip_ref, grads, weight_ref, out_ref, done_ref):
    cols, chans = plan.cols, plan.chans
    cells = clip_ref.shape[0]
    side = 2 * (spot_ref[1] & 1)
    taps = [(a, slot, b) for a in range(3) for slot, b in enumerate((1, side, 2 - side))]
    left = jnp.concatenate([grads[slot, (2 - a) * cols : (2 - a) * cols + cells] for a, slot, _ in taps], axis=1)
    acc = []
    for c in range(3):
        right = jnp.concatenate([weight_ref[a * 3 + b, c * chans : (c + 1) * chans] for a, _, b in taps], axis=1)
        acc.append(dot_nt(left, right))
    grad_act = acc[1]
    for c in (0, 2):
        grad_act = grad_act + shifted_rows(acc[c], 1 - c, cols)
    value = clip_ref[...].astype(F32)
    sig = 1.0 / (1.0 + jnp.exp(-value))
    own = grads[0, :cells].astype(F32)
    out_ref[...] = (own + grad_act * (sig * (1.0 + value * (1.0 - sig)))).astype(BF16)
    done_ref[...] = jnp.zeros_like(done_ref)


def shape(dims, dtype):
    return jax.ShapeDtypeStruct(dims, dtype)


def call(kernel, scalars, args, outs, scratch=(), us=1, limit=48, after=(), left=0):
    vmem, smem = pl.BlockSpec(memory_space=pltpu.VMEM), pl.BlockSpec(memory_space=pltpu.SMEM)
    hbm = pl.BlockSpec(memory_space=pltpu.HBM)
    args = [pltpu.with_memory_space_constraint(a, pltpu.HBM) for a in args[:left]] + list(args[left:])
    after = list(after)
    size = sum(a.size * a.dtype.itemsize for a in args)
    given = len(scalars) + len(args)

    def run(*refs):
        kernel(*refs[:given], *refs[given + len(after) :])

    return pl.pallas_call(
        run,
        out_shape=outs,
        in_specs=[smem] * len(scalars) + [hbm] * left + [vmem] * (len(args) - left) + [vmem] * len(after),
        out_specs=jax.tree.map(lambda _: vmem, outs),
        scratch_shapes=list(scratch),
        compiler_params=pltpu.CompilerParams(vmem_limit_bytes=limit * MIB),
        cost_estimate=pl.CostEstimate(flops=int(us * 1.15e9), bytes_accessed=size, transcendentals=0),
    )(*scalars, *args, *after)


class Plan:
    def __init__(self, count, cols, chans):
        nbits = count.bit_length() - 1
        self.cols, self.chans = cols, chans
        self.rows, self.down_rows = 27 * chans // count // 2, 3 * chans // count // 2
        self.group = math.gcd(16, math.gcd(self.rows, self.down_rows))
        self.lead = (2,) * (1 + nbits)
        links = [(0, 1)] + [(1, i) for i in range(nbits)]
        self.place = {link: (0 if link[0] == 0 else nbits - link[1]) for link in links}
        tops, tail = links[:3], links[3:]
        self.orders = [tops[g:] + tops[:g] + tail for g in range(3)]
        third = (self.rows + self.down_rows) // 3
        cut = third - self.down_rows
        self.cuts = [(0, cut), (cut, cut + third), (cut + third, self.rows)]

    def spot(self, h):
        nbits = len(self.lead) - 1
        return tuple(h >> (nbits - 1 - i) & 1 for i in range(nbits))

    def axis(self, g, step):
        order = self.orders[g]
        return sum(self.place[link] < self.place[order[step]] for link in order[step + 1 :])


def swapped(value, link):
    axis = ("tm", "height")[link[0]]
    return lax.ppermute(value, axis, [(i, i ^ (1 << link[1])) for i in range(lax.axis_size(axis))])


def body(clip, conv_weight, down_weight, grad_out):
    nframes, nrows, ncols, chans = clip.shape
    half = grad_out.shape[0]
    cells, span = nframes * ncols, half * ncols
    tm_count, count = lax.axis_size("tm"), lax.axis_size("height")
    plan = Plan(count, ncols, chans)
    spot = jnp.stack([lax.axis_index("tm"), lax.axis_index("height")]).astype(jnp.int32)
    mine = grad_out.reshape(span, chans)
    flat = clip.reshape(cells, chans)
    weight = conv_weight.reshape(9, 3 * chans, chans)
    core_link = (0, 0)
    part = chans // 2
    wide = 3 * part
    lead = plan.lead
    pair = 2 * span

    side = swapped(mine, (1, 0))
    here_other = swapped(mine, core_link)
    clip_other = swapped(flat, core_link)
    first = lax.ppermute(flat, "tm", [(i, i + 1) for i in range(1, tm_count - 1, 2)])
    second = lax.ppermute(clip_other, "tm", [(i, i + 3) for i in range(0, tm_count - 3, 2)])
    listed = (9, 3, part // plan.group, 2, plan.group, chans)
    turned, spread = call(
        functools.partial(weights_kernel, plan), [spot], [weight.reshape(listed), down_weight],
        [shape((9, chans, wide), BF16), shape((2 * wide, chans), BF16)],
        [pltpu.VMEM(listed[:3] + listed[4:], BF16), pltpu.VMEM(down_weight.shape, BF16), pltpu.SemaphoreType.DMA((10,))],
        us=3, limit=16, left=2,
    )
    far = lax.ppermute(
        side, "height", [(i, i + (2 if i % 2 == 0 else -2)) for i in range(count) if 0 <= i + (2 if i % 2 == 0 else -2) < count]
    )
    side_other = swapped(side, core_link)

    terms = [shape((3, wide, chans), F32), shape((chans, 3 * chans), F32)]
    even, odd, own_conv, own_sum, plus = call(
        functools.partial(own_kernel, plan), [spot],
        [flat, clip_other, first, second, mine, here_other, spread, turned],
        [shape((wide, 3 * cells // 2), BF16), shape((wide, 3 * cells // 2), BF16), *terms, shape((part, 3 * chans), F32)],
        [pltpu.VMEM((3 * cells, chans), BF16), pltpu.VMEM((pair, chans), BF16)], us=6, limit=20,
    )
    far, plus = lax.optimization_barrier((far, plus))
    far_other = swapped(far, core_link)
    side_conv, side_sum = call(
        functools.partial(side_kernel, plan), [spot], [side, side_other, even, odd, spread, turned], terms,
        [pltpu.VMEM((pair, chans), BF16)], us=2, limit=20,
    )
    outs = [shape((3, span, chans), BF16)]
    for begin, end in plan.cuts:
        outs += [shape(lead[1:] + (end - begin, part), BF16), shape(lead[1:] + (end - begin, part), F32)]
    down_dims = lead + (plan.down_rows, part)
    outs += [shape(down_dims, BF16), shape(down_dims, F32)]
    result = call(
        functools.partial(far_kernel, plan), [spot],
        [mine, side, far, far_other, even, odd, own_conv, own_sum, plus, side_conv, side_sum, spread, turned], outs,
        [pltpu.VMEM((pair, chans), BF16), pltpu.VMEM((3, wide, chans), F32), pltpu.VMEM(lead + (plan.rows, part), F32)],
        us=3, limit=20,
    )
    head = result[0]
    held = []
    for g in range(3):
        held += [result[2 + 2 * g], swapped(result[1 + 2 * g], plan.orders[g][0])]
    send, keep = call(
        functools.partial(single_kernel, plan, 0, 0), [spot], [result[8], swapped(result[7], core_link)],
        [shape(down_dims[1:], BF16), shape(down_dims[1:], F32)], limit=8,
    )
    down_held = [keep, swapped(send, plan.orders[0][0])]
    following = lax.ppermute(head, "tm", [(i + 1, i) for i in range(1, tm_count - 1, 2)])
    grads, ready = call(
        functools.partial(grads_kernel, plan), [spot],
        [mine, here_other, side, side_other, far, far_other, following, spread],
        [shape((3, (2 * half + 2) * ncols, chans), BF16), shape((8, part), F32)], us=1, limit=16,
    )
    grad_input, done = call(
        functools.partial(input_kernel, plan), [spot], [flat, grads, weight],
        [shape((cells, chans), BF16), shape((8, part), F32)], us=2, limit=24,
    )
    held = [held[:2] + down_held, held[2:4], held[4:6]]
    for step in (1, 2):
        for g in range(3):
            rows = plan.cuts[g][1] - plan.cuts[g][0] + (plan.down_rows if g == 0 else 0)
            dims = lead[step + 1 :] + (rows, part)
            send, keep = call(
                functools.partial(single_kernel, plan, g, step), [spot], held[g], [shape(dims, BF16), shape(dims, F32)],
                us=1, limit=8, after=[ready] if (g, step) == (2, 2) else (),
            )
            held[g] = [keep, swapped(send, plan.orders[g][step])]
    held = sum(held, [])
    for step in range(3, len(lead)):
        dims = lead[step + 1 :] + (plan.rows + plan.down_rows, part)
        send, keep = call(
            functools.partial(merge_kernel, plan, step), [spot], held, [shape(dims, BF16), shape(dims, F32)], limit=8,
            after=[done] if step == 3 else (),
        )
        held = [keep, swapped(send, plan.orders[0][step])]
    grad_conv, grad_down = call(
        functools.partial(join_kernel, plan), [spot], held + [swapped(v, core_link) for v in held],
        [shape((part // 2, 2 * plan.rows), F32), shape((part // 2, 2 * plan.down_rows), F32)],
        [pltpu.VMEM((part, 2 * plan.rows), F32), pltpu.VMEM((part, 2 * plan.down_rows), F32)],
        limit=8,
    )
    return (grad_input.reshape(clip.shape), grad_conv.T, grad_down.T)


def solution(mesh):
    placed = (P("tm", "height", None, None), P(), P(), P("tm", "height", None, None))
    return jax.shard_map(
        body,
        mesh=mesh,
        in_specs=placed,
        out_specs=(P("tm", "height", None, None), P("height", "tm"), P("height", "tm")),
        check_vma=False,
    )
```

```python
import functools
import math

import jax
import jax.numpy as jnp
from jax import lax
from jax.experimental import pallas as pl
from jax.experimental.pallas import tpu as pltpu
from jax.sharding import PartitionSpec as P

F32 = jnp.float32
BF16 = jnp.bfloat16
MIB = 1024 * 1024


def dot(left, right):
    return jnp.dot(left, right, preferred_element_type=F32)


def dot_nt(left, right):
    return lax.dot_general(left, right, (((1,), (1,)), ((), ())), preferred_element_type=F32)


def shifted_rows(value, step, period):
    if step == 0:
        return value
    rows = value.shape[0]
    moved = pltpu.roll(value, (-step) % rows, 0)
    place = lax.broadcasted_iota(jnp.int32, value.shape, 0) % period + step
    return jnp.where(jnp.logical_and(place >= 0, place < period), moved, 0.0)


def channel_of(place, group, core):
    return (place // group * 2 + core) * group + place % group


def one_hot(wanted, chans):
    dims = (wanted.shape[0], chans)
    return (lax.broadcasted_iota(jnp.int32, dims, 1) == wanted).astype(F32).astype(BF16)


def picker(chans, group, core):
    place = lax.broadcasted_iota(jnp.int32, (chans // 2, chans), 0)
    return one_hot(channel_of(place, group, core), chans)


def lay_pair(window, core, own, other, begin=0):
    size = own.shape[0]
    window[pl.ds(pl.multiple_of(begin + size * core, size), size)] = own[...]
    window[pl.ds(pl.multiple_of(begin + size * (1 - core), size), size)] = other[...]


def silu(value):
    return value / (1.0 + jnp.exp(-value))


def halved(lead, axis, index):
    rest = lead[:axis] + lead[axis + 1 :]
    for flat in range(math.prod(rest)):
        spot, left = [], flat
        for extent in reversed(rest):
            spot.insert(0, left % extent)
            left //= extent
        yield tuple(spot), tuple(spot[:axis]) + (index,) + tuple(spot[axis:])


def bit_of(spot_ref, link):
    return lax.shift_right_logical(spot_ref[link[0]], link[1]) & 1


def split_into(send, keep, lead, axis, mine, read):
    for to, where in halved(lead, axis, 1 - mine):
        send[to] = read(where).astype(send.dtype)
    for to, where in halved(lead, axis, mine):
        keep[to] = read(where)


def weights_kernel(plan, spot_ref, weight_ref, down_ref, turned_ref, spread_ref, weights, downs, sems):
    chans = plan.chans
    core = spot_ref[0] & 1
    copies = [pltpu.make_async_copy(down_ref, downs, sems.at[9])]
    copies += [pltpu.make_async_copy(weight_ref.at[ab, :, :, core], weights.at[ab], sems.at[ab]) for ab in range(9)]
    for copy in copies:
        copy.start()
    copies[0].wait()
    for k in range(3):
        spread_ref[k * chans : (k + 1) * chans] = downs[k].T
    for ab in range(9):
        copies[ab + 1].wait()
        block = weights[ab].reshape(3 * chans // 2, chans)
        turned_ref[ab] = block.T


def row_terms(plan, even, odd, cells, spread_ref, turned_ref, b, conv_ref):
    chans = plan.chans
    span = cells.shape[0]
    cross = []
    for s in range(5):
        begin = s // 2 * plan.cols
        cross.append(dot((even, odd)[s % 2][:, begin : begin + span], cells).astype(BF16))
    threes = [jnp.concatenate(cross[a : a + 3], axis=1) for a in range(3)]
    for a in range(3):
        conv_ref[a] = dot(threes[a], spread_ref[...])
    turned = jnp.concatenate([turned_ref[a * 3 + b] for a in range(3)], axis=1)
    down = dot(turned, jnp.concatenate(threes, axis=0))
    return down


def own_kernel(plan, spot_ref, clip_ref, clip_other, first_ref, second_ref, here_ref, here_other, spread_ref, turned_ref,
               even_ref, odd_ref, conv_ref, sum_ref, plus_ref, clips, cells):
    cols, chans = plan.cols, plan.chans
    part = chans // 2
    core = spot_ref[0] & 1
    rows = clip_ref.shape[0]
    clips[:rows] = first_ref[...] + second_ref[...]
    lay_pair(clips, core, clip_ref, clip_other, rows)
    lay_pair(cells, core, here_ref, here_other)
    pick = picker(chans, plan.group, core)
    plain = dot_nt(pick, clips[...])
    chosen = silu(plain).astype(BF16).astype(F32)
    plain = plain.astype(BF16)
    steps = lax.broadcasted_iota(jnp.int32, chosen.shape, 1) % cols
    count = 3 * rows // cols // 2
    for c in range(3):
        moved = chosen
        if c != 1:
            moved = pltpu.roll(chosen, (1 - c) % chosen.shape[1], 1)
            moved = jnp.where(steps == (0 if c == 0 else cols - 1), 0.0, moved)
        moved = moved.astype(BF16)
        lanes = slice(c * part, (c + 1) * part)
        for f in range(count):
            to = slice(f * cols, (f + 1) * cols)
            even_ref[lanes, to] = moved[:, 2 * f * cols : (2 * f + 1) * cols]
            odd_ref[lanes, to] = moved[:, (2 * f + 1) * cols : (2 * f + 2) * cols]
    here = cells[...]
    for k in range(3):
        halves = [plain[:, (2 * f + k % 2) * cols : (2 * f + k % 2 + 1) * cols] for f in range(count)]
        begin = 1 + k // 2
        frames = jnp.concatenate(halves[begin : begin + here.shape[0] // cols], axis=1)
        plus_ref[:, k * chans : (k + 1) * chans] = dot(frames, here)
    sum_ref[...] = row_terms(plan, even_ref, odd_ref, here, spread_ref, turned_ref, 1, conv_ref)


def side_kernel(plan, spot_ref, side_ref, side_other, even_ref, odd_ref, spread_ref, turned_ref, conv_ref, sum_ref, cells):
    lay_pair(cells, spot_ref[0] & 1, side_ref, side_other)
    b = 2 * (spot_ref[1] & 1)
    sum_ref[...] = row_terms(plan, even_ref, odd_ref, cells[...], spread_ref, turned_ref, b, conv_ref)


def far_kernel(plan, spot_ref, here_ref, side_ref, far_ref, far_other, even_ref, odd_ref, own_conv, own_sum, plus_ref, side_conv,
               side_sum, spread_ref, turned_ref, head_ref, *rest):
    outs, (cells, conv, total) = rest[:-3], rest[-3:]
    chans = plan.chans
    part = chans // 2
    core = spot_ref[0] & 1
    odd_row = spot_ref[1] & 1
    lay_pair(cells, core, far_ref, far_other)
    down = row_terms(plan, even_ref, odd_ref, cells[...], spread_ref, turned_ref, 2 - 2 * odd_row, conv)
    down = own_sum[...] + side_sum[...] + down
    for slot, ref in enumerate((here_ref, side_ref, far_ref)):
        head_ref[slot] = ref[...]
    wide = 3 * part

    def place(a, b, value):
        first = (a * 3 + b) * wide
        begin = first
        while begin < first + wide:
            h = begin // plan.rows
            end = min((h + 1) * plan.rows, first + wide)
            for y in range(2):
                total[(y,) + plan.spot(h) + (slice(begin - h * plan.rows, end - h * plan.rows),)] = value[
                    begin - first : end - first, y * part : (y + 1) * part
                ]
            begin = end

    for a in range(3):
        place(a, 1, own_conv[a])
    for parity in range(2):
        @pl.when(odd_row == parity)
        def _():
            for a in range(3):
                place(a, 2 * parity, side_conv[a])
                place(a, 2 - 2 * parity, conv[a])
    for g in range(3):
        link = plan.orders[g][0]
        begin, end = plan.cuts[g]
        split_into(
            outs[2 * g], outs[2 * g + 1], plan.lead, plan.axis(g, 0), bit_of(spot_ref, link),
            lambda where: total[where + (slice(begin, end),)],
        )
    mine = core == 0
    pairs = range(0, chans, 2 * plan.group)
    low = jnp.concatenate([down[i : i + plan.group] for i in pairs], axis=0)
    high = jnp.concatenate([down[i + plan.group : i + 2 * plan.group] for i in pairs], axis=0)
    keep = jnp.where(mine, low, high) + plus_ref[...]
    for ref, value in ((outs[6], jnp.where(mine, high, low)), (outs[7], keep)):
        for h in range(math.prod(plan.lead[1:])):
            begin = h * plan.down_rows
            while begin < (h + 1) * plan.down_rows:
                k = begin // part
                end = min((k + 1) * part, (h + 1) * plan.down_rows)
                for y in range(2):
                    ref[(y,) + plan.spot(h) + (slice(begin - h * plan.down_rows, end - h * plan.down_rows),)] = value[
                        begin - k * part : end - k * part, k * chans + y * part : k * chans + (y + 1) * part
                    ].astype(ref.dtype)
                begin = end


def merge_kernel(plan, step, spot_ref, *refs):
    ins, (send, keep) = refs[:-2], refs[-2:]

    def read(where):
        return jnp.concatenate([ins[i][where] + ins[i + 1][where].astype(F32) for i in range(0, len(ins), 2)], axis=0)

    split_into(send, keep, plan.lead[step:], plan.axis(0, step), bit_of(spot_ref, plan.orders[0][step]), read)


def single_kernel(plan, g, step, spot_ref, *refs):
    ins, (send, keep) = refs[:-2], refs[-2:]

    def read(where):
        pieces = [ins[i][where] + ins[i + 1][where].astype(F32) for i in range(0, len(ins), 2)]
        return pieces[0] if len(pieces) == 1 else jnp.concatenate(pieces, axis=0)

    split_into(send, keep, plan.lead[step:], plan.axis(g, step), bit_of(spot_ref, plan.orders[g][step]), read)


def join_kernel(plan, spot_ref, held, got, held_other, got_other, conv_ref, down_ref, turned, down_turned):
    core = spot_ref[0] & 1
    group = plan.group
    rows, down_rows = plan.rows, plan.down_rows
    own = held[...] + got[...].astype(F32)
    other = held_other[...] + got_other[...].astype(F32)
    first, second = jnp.where(core == 0, own, other), jnp.where(core == 0, other, own)

    def merged(begin, end):
        pieces = []
        for at in range(begin, end, group):
            pieces += [first[at : at + group], second[at : at + group]]
        return pieces

    cut = plan.cuts[0][1]
    conv = merged(0, cut) + merged(cut + down_rows, rows + down_rows)
    down = merged(cut, cut + down_rows)
    width = own.shape[1] // 2
    for ref, pieces, space in ((conv_ref, conv, turned), (down_ref, down, down_turned)):
        space[...] = jnp.concatenate(pieces, axis=0).T
        ref[...] = space[pl.ds(pl.multiple_of(core * width, width), width)]


def grads_kernel(plan, spot_ref, here_ref, here_other, side_ref, side_other, far_ref, far_other, next_ref, spread_ref, grads, done_ref):
    cols, chans = plan.cols, plan.chans
    half = side_ref.shape[0] // cols
    core = spot_ref[0] & 1
    rows = ((here_ref, here_other), (side_ref, side_other), (far_ref, far_other))
    for slot, (own, other) in enumerate(rows):
        following = jnp.where(core == 0, other[...], next_ref[slot])
        every = jnp.concatenate([own[...], following], axis=0)
        here = every[: (half + 1) * cols]
        after = every[cols : (half + 2) * cols]
        even = (dot(after, spread_ref[:chans]) + dot(here, spread_ref[2 * chans :])).astype(BF16)
        odd = dot(after, spread_ref[chans : 2 * chans]).astype(BF16)
        for u in range(half + 1):
            grads[slot, 2 * u * cols : (2 * u + 1) * cols] = even[u * cols : (u + 1) * cols]
            grads[slot, (2 * u + 1) * cols : (2 * u + 2) * cols] = odd[u * cols : (u + 1) * cols]
    done_ref[...] = jnp.zeros_like(done_ref)


def input_kernel(plan, spot_ref, clip_ref, grads, weight_ref, out_ref, done_ref):
    cols, chans = plan.cols, plan.chans
    cells = clip_ref.shape[0]
    side = 2 * (spot_ref[1] & 1)
    taps = [(a, slot, b) for a in range(3) for slot, b in enumerate((1, side, 2 - side))]
    left = jnp.concatenate([grads[slot, (2 - a) * cols : (2 - a) * cols + cells] for a, slot, _ in taps], axis=1)
    acc = []
    for c in range(3):
        right = jnp.concatenate([weight_ref[a * 3 + b, c * chans : (c + 1) * chans] for a, _, b in taps], axis=1)
        acc.append(dot_nt(left, right))
    grad_act = acc[1]
    for c in (0, 2):
        grad_act = grad_act + shifted_rows(acc[c], 1 - c, cols)
    value = clip_ref[...].astype(F32)
    sig = 1.0 / (1.0 + jnp.exp(-value))
    own = grads[0, :cells].astype(F32)
    out_ref[...] = (own + grad_act * (sig * (1.0 + value * (1.0 - sig)))).astype(BF16)
    done_ref[...] = jnp.zeros_like(done_ref)


def shape(dims, dtype):
    return jax.ShapeDtypeStruct(dims, dtype)


def call(kernel, scalars, args, outs, scratch=(), us=1, limit=48, after=(), left=0):
    vmem, smem = pl.BlockSpec(memory_space=pltpu.VMEM), pl.BlockSpec(memory_space=pltpu.SMEM)
    hbm = pl.BlockSpec(memory_space=pltpu.HBM)
    args = [pltpu.with_memory_space_constraint(a, pltpu.HBM) for a in args[:left]] + list(args[left:])
    after = list(after)
    size = sum(a.size * a.dtype.itemsize for a in args)
    given = len(scalars) + len(args)

    def run(*refs):
        kernel(*refs[:given], *refs[given + len(after) :])

    return pl.pallas_call(
        run,
        out_shape=outs,
        in_specs=[smem] * len(scalars) + [hbm] * left + [vmem] * (len(args) - left) + [vmem] * len(after),
        out_specs=jax.tree.map(lambda _: vmem, outs),
        scratch_shapes=list(scratch),
        compiler_params=pltpu.CompilerParams(vmem_limit_bytes=limit * MIB),
        cost_estimate=pl.CostEstimate(flops=int(us * 1.15e9), bytes_accessed=size, transcendentals=0),
    )(*scalars, *args, *after)


class Plan:
    def __init__(self, count, cols, chans):
        nbits = count.bit_length() - 1
        self.cols, self.chans = cols, chans
        self.rows, self.down_rows = 27 * chans // count // 2, 3 * chans // count // 2
        self.group = math.gcd(16, math.gcd(self.rows, self.down_rows))
        self.lead = (2,) * (1 + nbits)
        links = [(0, 1)] + [(1, i) for i in range(nbits)]
        self.place = {link: (0 if link[0] == 0 else nbits - link[1]) for link in links}
        tops, tail = links[:3], links[3:]
        self.orders = [tops[g:] + tops[:g] + tail for g in range(3)]
        third = (self.rows + self.down_rows) // 3
        cut = third - self.down_rows
        self.cuts = [(0, cut), (cut, cut + third), (cut + third, self.rows)]

    def spot(self, h):
        nbits = len(self.lead) - 1
        return tuple(h >> (nbits - 1 - i) & 1 for i in range(nbits))

    def axis(self, g, step):
        order = self.orders[g]
        return sum(self.place[link] < self.place[order[step]] for link in order[step + 1 :])


def swapped(value, link):
    axis = ("tm", "height")[link[0]]
    return lax.ppermute(value, axis, [(i, i ^ (1 << link[1])) for i in range(lax.axis_size(axis))])


def body(clip, conv_weight, down_weight, grad_out):
    nframes, nrows, ncols, chans = clip.shape
    half = grad_out.shape[0]
    cells, span = nframes * ncols, half * ncols
    tm_count, count = lax.axis_size("tm"), lax.axis_size("height")
    plan = Plan(count, ncols, chans)
    spot = jnp.stack([lax.axis_index("tm"), lax.axis_index("height")]).astype(jnp.int32)
    mine = grad_out.reshape(span, chans)
    flat = clip.reshape(cells, chans)
    weight = conv_weight.reshape(9, 3 * chans, chans)
    core_link = (0, 0)
    part = chans // 2
    wide = 3 * part
    lead = plan.lead
    pair = 2 * span

    side = swapped(mine, (1, 0))
    here_other = swapped(mine, core_link)
    clip_other = swapped(flat, core_link)
    first = lax.ppermute(flat, "tm", [(i, i + 1) for i in range(1, tm_count - 1, 2)])
    second = lax.ppermute(clip_other, "tm", [(i, i + 3) for i in range(0, tm_count - 3, 2)])
    listed = (9, 3, part // plan.group, 2, plan.group, chans)
    turned, spread = call(
        functools.partial(weights_kernel, plan), [spot], [weight.reshape(listed), down_weight],
        [shape((9, chans, wide), BF16), shape((2 * wide, chans), BF16)],
        [pltpu.VMEM(listed[:3] + listed[4:], BF16), pltpu.VMEM(down_weight.shape, BF16), pltpu.SemaphoreType.DMA((10,))],
        us=3, limit=16, left=2,
    )
    far = lax.ppermute(
        side, "height", [(i, i + (2 if i % 2 == 0 else -2)) for i in range(count) if 0 <= i + (2 if i % 2 == 0 else -2) < count]
    )
    side_other = swapped(side, core_link)

    terms = [shape((3, wide, chans), F32), shape((chans, 3 * chans), F32)]
    even, odd, own_conv, own_sum, plus = call(
        functools.partial(own_kernel, plan), [spot],
        [flat, clip_other, first, second, mine, here_other, spread, turned],
        [shape((wide, 3 * cells // 2), BF16), shape((wide, 3 * cells // 2), BF16), *terms, shape((part, 3 * chans), F32)],
        [pltpu.VMEM((3 * cells, chans), BF16), pltpu.VMEM((pair, chans), BF16)], us=6, limit=20,
    )
    far, plus = lax.optimization_barrier((far, plus))
    far_other = swapped(far, core_link)
    side_conv, side_sum = call(
        functools.partial(side_kernel, plan), [spot], [side, side_other, even, odd, spread, turned], terms,
        [pltpu.VMEM((pair, chans), BF16)], us=2, limit=20,
    )
    outs = [shape((3, span, chans), BF16)]
    for begin, end in plan.cuts:
        outs += [shape(lead[1:] + (end - begin, part), BF16), shape(lead[1:] + (end - begin, part), F32)]
    down_dims = lead + (plan.down_rows, part)
    outs += [shape(down_dims, BF16), shape(down_dims, F32)]
    result = call(
        functools.partial(far_kernel, plan), [spot],
        [mine, side, far, far_other, even, odd, own_conv, own_sum, plus, side_conv, side_sum, spread, turned], outs,
        [pltpu.VMEM((pair, chans), BF16), pltpu.VMEM((3, wide, chans), F32), pltpu.VMEM(lead + (plan.rows, part), F32)],
        us=3, limit=20,
    )
    head = result[0]
    held = []
    for g in range(3):
        held += [result[2 + 2 * g], swapped(result[1 + 2 * g], plan.orders[g][0])]
    send, keep = call(
        functools.partial(single_kernel, plan, 0, 0), [spot], [result[8], swapped(result[7], core_link)],
        [shape(down_dims[1:], BF16), shape(down_dims[1:], F32)], limit=8,
    )
    down_held = [keep, swapped(send, plan.orders[0][0])]
    following = lax.ppermute(head, "tm", [(i + 1, i) for i in range(1, tm_count - 1, 2)])
    grads, ready = call(
        functools.partial(grads_kernel, plan), [spot],
        [mine, here_other, side, side_other, far, far_other, following, spread],
        [shape((3, (2 * half + 2) * ncols, chans), BF16), shape((8, part), F32)], us=1, limit=16,
    )
    grad_input, done = call(
        functools.partial(input_kernel, plan), [spot], [flat, grads, weight],
        [shape((cells, chans), BF16), shape((8, part), F32)], us=2, limit=24,
    )
    held = [held[:2] + down_held, held[2:4], held[4:6]]
    for step in (1, 2):
        for g in range(3):
            rows = plan.cuts[g][1] - plan.cuts[g][0] + (plan.down_rows if g == 0 else 0)
            dims = lead[step + 1 :] + (rows, part)
            send, keep = call(
                functools.partial(single_kernel, plan, g, step), [spot], held[g], [shape(dims, BF16), shape(dims, F32)],
                us=1, limit=8, after=[ready] if (g, step) == (2, 2) else (),
            )
            held[g] = [keep, swapped(send, plan.orders[g][step])]
    held = sum(held, [])
    for step in range(3, len(lead)):
        dims = lead[step + 1 :] + (plan.rows + plan.down_rows, part)
        send, keep = call(
            functools.partial(merge_kernel, plan, step), [spot], held, [shape(dims, BF16), shape(dims, F32)], limit=8,
        )
        held = [keep, swapped(send, plan.orders[0][step])]
    arrived, done = lax.optimization_barrier((held[1], done))
    grad_conv, grad_down = call(
        functools.partial(join_kernel, plan), [spot], held + [swapped(held[0], core_link), swapped(arrived, core_link)],
        [shape((part // 2, 2 * plan.rows), F32), shape((part // 2, 2 * plan.down_rows), F32)],
        [pltpu.VMEM((part, 2 * plan.rows), F32), pltpu.VMEM((part, 2 * plan.down_rows), F32)],
        limit=8, after=[done],
    )
    return (grad_input.reshape(clip.shape), grad_conv.T, grad_down.T)


def solution(mesh):
    placed = (P("tm", "height", None, None), P(), P(), P("tm", "height", None, None))
    return jax.shard_map(
        body,
        mesh=mesh,
        in_specs=placed,
        out_specs=(P("tm", "height", None, None), P("height", "tm"), P("height", "tm")),
        check_vma=False,
    )
```

```python
import functools
import math

import jax
import jax.numpy as jnp
from jax import lax
from jax.experimental import pallas as pl
from jax.experimental.pallas import tpu as pltpu
from jax.sharding import PartitionSpec as P

F32 = jnp.float32
BF16 = jnp.bfloat16
MIB = 1024 * 1024


def dot(left, right):
    return jnp.dot(left, right, preferred_element_type=F32)


def dot_nt(left, right):
    return lax.dot_general(left, right, (((1,), (1,)), ((), ())), preferred_element_type=F32)


def shifted_rows(value, step, period):
    if step == 0:
        return value
    rows = value.shape[0]
    moved = pltpu.roll(value, (-step) % rows, 0)
    place = lax.broadcasted_iota(jnp.int32, value.shape, 0) % period + step
    return jnp.where(jnp.logical_and(place >= 0, place < period), moved, 0.0)


def channel_of(place, group, core):
    return (place // group * 2 + core) * group + place % group


def one_hot(wanted, chans):
    dims = (wanted.shape[0], chans)
    return (lax.broadcasted_iota(jnp.int32, dims, 1) == wanted).astype(F32).astype(BF16)


def picker(chans, group, core):
    place = lax.broadcasted_iota(jnp.int32, (chans // 2, chans), 0)
    return one_hot(channel_of(place, group, core), chans)


def lay_pair(window, core, own, other, begin=0):
    size = own.shape[0]
    window[pl.ds(pl.multiple_of(begin + size * core, size), size)] = own[...]
    window[pl.ds(pl.multiple_of(begin + size * (1 - core), size), size)] = other[...]


def silu(value):
    return value / (1.0 + jnp.exp(-value))


def halved(lead, axis, index):
    rest = lead[:axis] + lead[axis + 1 :]
    for flat in range(math.prod(rest)):
        spot, left = [], flat
        for extent in reversed(rest):
            spot.insert(0, left % extent)
            left //= extent
        yield tuple(spot), tuple(spot[:axis]) + (index,) + tuple(spot[axis:])


def bit_of(spot_ref, link):
    return lax.shift_right_logical(spot_ref[link[0]], link[1]) & 1


def split_into(send, keep, lead, axis, mine, read):
    for to, where in halved(lead, axis, 1 - mine):
        send[to] = read(where).astype(send.dtype)
    for to, where in halved(lead, axis, mine):
        keep[to] = read(where)


def weights_kernel(plan, spot_ref, weight_ref, down_ref, turned_ref, spread_ref, weights, downs, sems):
    chans = plan.chans
    core = spot_ref[0] & 1
    copies = [pltpu.make_async_copy(down_ref, downs, sems.at[9])]
    copies += [pltpu.make_async_copy(weight_ref.at[ab, :, :, core], weights.at[ab], sems.at[ab]) for ab in range(9)]
    for copy in copies:
        copy.start()
    copies[0].wait()
    for k in range(3):
        spread_ref[k * chans : (k + 1) * chans] = downs[k].T
    for ab in range(9):
        copies[ab + 1].wait()
        block = weights[ab].reshape(3 * chans // 2, chans)
        turned_ref[ab] = block.T


def row_terms(plan, even, odd, cells, spread_ref, turned_ref, b, conv_ref):
    chans = plan.chans
    span = cells.shape[0]
    cross = []
    for s in range(5):
        begin = s // 2 * plan.cols
        cross.append(dot((even, odd)[s % 2][:, begin : begin + span], cells).astype(BF16))
    threes = [jnp.concatenate(cross[a : a + 3], axis=1) for a in range(3)]
    for a in range(3):
        conv_ref[a] = dot(threes[a], spread_ref[...])
    turned = jnp.concatenate([turned_ref[a * 3 + b] for a in range(3)], axis=1)
    down = dot(turned, jnp.concatenate(threes, axis=0))
    return down


def own_kernel(plan, spot_ref, clip_ref, clip_other, first_ref, second_ref, here_ref, here_other, spread_ref, turned_ref,
               even_ref, odd_ref, conv_ref, sum_ref, plus_ref, clips, cells):
    cols, chans = plan.cols, plan.chans
    part = chans // 2
    core = spot_ref[0] & 1
    rows = clip_ref.shape[0]
    clips[:rows] = first_ref[...] + second_ref[...]
    lay_pair(clips, core, clip_ref, clip_other, rows)
    lay_pair(cells, core, here_ref, here_other)
    pick = picker(chans, plan.group, core)
    plain = dot_nt(pick, clips[...])
    chosen = silu(plain).astype(BF16).astype(F32)
    plain = plain.astype(BF16)
    steps = lax.broadcasted_iota(jnp.int32, chosen.shape, 1) % cols
    count = 3 * rows // cols // 2
    for c in range(3):
        moved = chosen
        if c != 1:
            moved = pltpu.roll(chosen, (1 - c) % chosen.shape[1], 1)
            moved = jnp.where(steps == (0 if c == 0 else cols - 1), 0.0, moved)
        moved = moved.astype(BF16)
        lanes = slice(c * part, (c + 1) * part)
        for f in range(count):
            to = slice(f * cols, (f + 1) * cols)
            even_ref[lanes, to] = moved[:, 2 * f * cols : (2 * f + 1) * cols]
            odd_ref[lanes, to] = moved[:, (2 * f + 1) * cols : (2 * f + 2) * cols]
    here = cells[...]
    for k in range(3):
        halves = [plain[:, (2 * f + k % 2) * cols : (2 * f + k % 2 + 1) * cols] for f in range(count)]
        begin = 1 + k // 2
        frames = jnp.concatenate(halves[begin : begin + here.shape[0] // cols], axis=1)
        plus_ref[:, k * chans : (k + 1) * chans] = dot(frames, here)
    sum_ref[...] = row_terms(plan, even_ref, odd_ref, here, spread_ref, turned_ref, 1, conv_ref)


def side_kernel(plan, spot_ref, side_ref, side_other, even_ref, odd_ref, spread_ref, turned_ref, conv_ref, sum_ref, cells):
    lay_pair(cells, spot_ref[0] & 1, side_ref, side_other)
    b = 2 * (spot_ref[1] & 1)
    sum_ref[...] = row_terms(plan, even_ref, odd_ref, cells[...], spread_ref, turned_ref, b, conv_ref)


def far_kernel(plan, spot_ref, here_ref, side_ref, far_ref, far_other, even_ref, odd_ref, own_conv, own_sum, plus_ref, side_conv,
               side_sum, spread_ref, turned_ref, head_ref, *rest):
    outs, (cells, conv, total) = rest[:-3], rest[-3:]
    chans = plan.chans
    part = chans // 2
    core = spot_ref[0] & 1
    odd_row = spot_ref[1] & 1
    lay_pair(cells, core, far_ref, far_other)
    down = row_terms(plan, even_ref, odd_ref, cells[...], spread_ref, turned_ref, 2 - 2 * odd_row, conv)
    down = own_sum[...] + side_sum[...] + down
    for slot, ref in enumerate((here_ref, side_ref, far_ref)):
        head_ref[slot] = ref[...]
    wide = 3 * part

    def place(a, b, value):
        first = (a * 3 + b) * wide
        begin = first
        while begin < first + wide:
            h = begin // plan.rows
            end = min((h + 1) * plan.rows, first + wide)
            for y in range(2):
                total[(y,) + plan.spot(h) + (slice(begin - h * plan.rows, end - h * plan.rows),)] = value[
                    begin - first : end - first, y * part : (y + 1) * part
                ]
            begin = end

    for a in range(3):
        place(a, 1, own_conv[a])
    for parity in range(2):
        @pl.when(odd_row == parity)
        def _():
            for a in range(3):
                place(a, 2 * parity, side_conv[a])
                place(a, 2 - 2 * parity, conv[a])
    for g in range(3):
        link = plan.orders[g][0]
        begin, end = plan.cuts[g]
        split_into(
            outs[2 * g], outs[2 * g + 1], plan.lead, plan.axis(g, 0), bit_of(spot_ref, link),
            lambda where: total[where + (slice(begin, end),)],
        )
    mine = core == 0
    pairs = range(0, chans, 2 * plan.group)
    low = jnp.concatenate([down[i : i + plan.group] for i in pairs], axis=0)
    high = jnp.concatenate([down[i + plan.group : i + 2 * plan.group] for i in pairs], axis=0)
    keep = jnp.where(mine, low, high) + plus_ref[...]
    for ref, value in ((outs[6], jnp.where(mine, high, low)), (outs[7], keep)):
        for h in range(math.prod(plan.lead[1:])):
            begin = h * plan.down_rows
            while begin < (h + 1) * plan.down_rows:
                k = begin // part
                end = min((k + 1) * part, (h + 1) * plan.down_rows)
                for y in range(2):
                    ref[(y,) + plan.spot(h) + (slice(begin - h * plan.down_rows, end - h * plan.down_rows),)] = value[
                        begin - k * part : end - k * part, k * chans + y * part : k * chans + (y + 1) * part
                    ].astype(ref.dtype)
                begin = end


def merge_kernel(plan, step, spot_ref, *refs):
    ins, (send, keep) = refs[:-2], refs[-2:]

    def read(where):
        return jnp.concatenate([ins[i][where] + ins[i + 1][where].astype(F32) for i in range(0, len(ins), 2)], axis=0)

    split_into(send, keep, plan.lead[step:], plan.axis(0, step), bit_of(spot_ref, plan.orders[0][step]), read)


def single_kernel(plan, g, step, spot_ref, *refs):
    ins, (send, keep) = refs[:-2], refs[-2:]

    def read(where):
        pieces = [ins[i][where] + ins[i + 1][where].astype(F32) for i in range(0, len(ins), 2)]
        return pieces[0] if len(pieces) == 1 else jnp.concatenate(pieces, axis=0)

    split_into(send, keep, plan.lead[step:], plan.axis(g, step), bit_of(spot_ref, plan.orders[g][step]), read)


def join_kernel(plan, spot_ref, held, got, held_other, got_other, conv_ref, down_ref, turned, down_turned):
    core = spot_ref[0] & 1
    group = plan.group
    rows, down_rows = plan.rows, plan.down_rows
    own = held[...] + got[...].astype(F32)
    other = held_other[...] + got_other[...].astype(F32)
    first, second = jnp.where(core == 0, own, other), jnp.where(core == 0, other, own)

    def merged(begin, end):
        pieces = []
        for at in range(begin, end, group):
            pieces += [first[at : at + group], second[at : at + group]]
        return pieces

    cut = plan.cuts[0][1]
    conv = merged(0, cut) + merged(cut + down_rows, rows + down_rows)
    down = merged(cut, cut + down_rows)
    width = own.shape[1] // 2
    for ref, pieces, space in ((conv_ref, conv, turned), (down_ref, down, down_turned)):
        space[...] = jnp.concatenate(pieces, axis=0).T
        ref[...] = space[pl.ds(pl.multiple_of(core * width, width), width)]


def grads_kernel(plan, spot_ref, here_ref, here_other, side_ref, side_other, far_ref, far_other, next_ref, spread_ref, grads, done_ref):
    cols, chans = plan.cols, plan.chans
    half = side_ref.shape[0] // cols
    core = spot_ref[0] & 1
    rows = ((here_ref, here_other), (side_ref, side_other), (far_ref, far_other))
    for slot, (own, other) in enumerate(rows):
        following = jnp.where(core == 0, other[...], next_ref[slot])
        every = jnp.concatenate([own[...], following], axis=0)
        here = every[: (half + 1) * cols]
        after = every[cols : (half + 2) * cols]
        even = (dot(after, spread_ref[:chans]) + dot(here, spread_ref[2 * chans :])).astype(BF16)
        odd = dot(after, spread_ref[chans : 2 * chans]).astype(BF16)
        for u in range(half + 1):
            grads[slot, 2 * u * cols : (2 * u + 1) * cols] = even[u * cols : (u + 1) * cols]
            grads[slot, (2 * u + 1) * cols : (2 * u + 2) * cols] = odd[u * cols : (u + 1) * cols]
    done_ref[...] = jnp.zeros_like(done_ref)


def tap_sum(plan, side, grads, weight_ref, cells, c):
    cols, chans = plan.cols, plan.chans
    taps = [(a, slot, b) for a in range(3) for slot, b in enumerate((1, side, 2 - side))]
    left = jnp.concatenate([grads[slot, (2 - a) * cols : (2 - a) * cols + cells] for a, slot, _ in taps], axis=1)
    right = jnp.concatenate([weight_ref[a * 3 + b, c * chans : (c + 1) * chans] for a, _, b in taps], axis=1)
    return dot_nt(left, right)


def middle_kernel(plan, spot_ref, grads, weight_ref, middle_ref, done_ref):
    middle_ref[...] = tap_sum(plan, 2 * (spot_ref[1] & 1), grads, weight_ref, middle_ref.shape[0], 1)
    done_ref[...] = jnp.zeros_like(done_ref)


def input_kernel(plan, spot_ref, clip_ref, grads, middle_ref, weight_ref, out_ref, done_ref):
    cols, chans = plan.cols, plan.chans
    cells = clip_ref.shape[0]
    side = 2 * (spot_ref[1] & 1)
    acc = {c: tap_sum(plan, side, grads, weight_ref, cells, c) for c in (0, 2)}
    grad_act = middle_ref[...]
    for c in (0, 2):
        grad_act = grad_act + shifted_rows(acc[c], 1 - c, cols)
    value = clip_ref[...].astype(F32)
    sig = 1.0 / (1.0 + jnp.exp(-value))
    own = grads[0, :cells].astype(F32)
    out_ref[...] = (own + grad_act * (sig * (1.0 + value * (1.0 - sig)))).astype(BF16)
    done_ref[...] = jnp.zeros_like(done_ref)


def shape(dims, dtype):
    return jax.ShapeDtypeStruct(dims, dtype)


def call(kernel, scalars, args, outs, scratch=(), us=1, limit=48, after=(), left=0):
    vmem, smem = pl.BlockSpec(memory_space=pltpu.VMEM), pl.BlockSpec(memory_space=pltpu.SMEM)
    hbm = pl.BlockSpec(memory_space=pltpu.HBM)
    args = [pltpu.with_memory_space_constraint(a, pltpu.HBM) for a in args[:left]] + list(args[left:])
    after = list(after)
    size = sum(a.size * a.dtype.itemsize for a in args)
    given = len(scalars) + len(args)

    def run(*refs):
        kernel(*refs[:given], *refs[given + len(after) :])

    return pl.pallas_call(
        run,
        out_shape=outs,
        in_specs=[smem] * len(scalars) + [hbm] * left + [vmem] * (len(args) - left) + [vmem] * len(after),
        out_specs=jax.tree.map(lambda _: vmem, outs),
        scratch_shapes=list(scratch),
        compiler_params=pltpu.CompilerParams(vmem_limit_bytes=limit * MIB),
        cost_estimate=pl.CostEstimate(flops=int(us * 1.15e9), bytes_accessed=size, transcendentals=0),
    )(*scalars, *args, *after)


class Plan:
    def __init__(self, count, cols, chans):
        nbits = count.bit_length() - 1
        self.cols, self.chans = cols, chans
        self.rows, self.down_rows = 27 * chans // count // 2, 3 * chans // count // 2
        self.group = math.gcd(16, math.gcd(self.rows, self.down_rows))
        self.lead = (2,) * (1 + nbits)
        links = [(0, 1)] + [(1, i) for i in range(nbits)]
        self.place = {link: (0 if link[0] == 0 else nbits - link[1]) for link in links}
        tops, tail = links[:3], links[3:]
        self.orders = [tops[g:] + tops[:g] + tail for g in range(3)]
        third = (self.rows + self.down_rows) // 3
        cut = third - self.down_rows
        self.cuts = [(0, cut), (cut, cut + third), (cut + third, self.rows)]

    def spot(self, h):
        nbits = len(self.lead) - 1
        return tuple(h >> (nbits - 1 - i) & 1 for i in range(nbits))

    def axis(self, g, step):
        order = self.orders[g]
        return sum(self.place[link] < self.place[order[step]] for link in order[step + 1 :])


def swapped(value, link):
    axis = ("tm", "height")[link[0]]
    return lax.ppermute(value, axis, [(i, i ^ (1 << link[1])) for i in range(lax.axis_size(axis))])


def body(clip, conv_weight, down_weight, grad_out):
    nframes, nrows, ncols, chans = clip.shape
    half = grad_out.shape[0]
    cells, span = nframes * ncols, half * ncols
    tm_count, count = lax.axis_size("tm"), lax.axis_size("height")
    plan = Plan(count, ncols, chans)
    spot = jnp.stack([lax.axis_index("tm"), lax.axis_index("height")]).astype(jnp.int32)
    mine = grad_out.reshape(span, chans)
    flat = clip.reshape(cells, chans)
    weight = conv_weight.reshape(9, 3 * chans, chans)
    core_link = (0, 0)
    part = chans // 2
    wide = 3 * part
    lead = plan.lead
    pair = 2 * span

    side = swapped(mine, (1, 0))
    here_other = swapped(mine, core_link)
    clip_other = swapped(flat, core_link)
    first = lax.ppermute(flat, "tm", [(i, i + 1) for i in range(1, tm_count - 1, 2)])
    second = lax.ppermute(clip_other, "tm", [(i, i + 3) for i in range(0, tm_count - 3, 2)])
    listed = (9, 3, part // plan.group, 2, plan.group, chans)
    turned, spread = call(
        functools.partial(weights_kernel, plan), [spot], [weight.reshape(listed), down_weight],
        [shape((9, chans, wide), BF16), shape((2 * wide, chans), BF16)],
        [pltpu.VMEM(listed[:3] + listed[4:], BF16), pltpu.VMEM(down_weight.shape, BF16), pltpu.SemaphoreType.DMA((10,))],
        us=3, limit=16, left=2,
    )
    far = lax.ppermute(
        side, "height", [(i, i + (2 if i % 2 == 0 else -2)) for i in range(count) if 0 <= i + (2 if i % 2 == 0 else -2) < count]
    )
    side_other = swapped(side, core_link)

    terms = [shape((3, wide, chans), F32), shape((chans, 3 * chans), F32)]
    even, odd, own_conv, own_sum, plus = call(
        functools.partial(own_kernel, plan), [spot],
        [flat, clip_other, first, second, mine, here_other, spread, turned],
        [shape((wide, 3 * cells // 2), BF16), shape((wide, 3 * cells // 2), BF16), *terms, shape((part, 3 * chans), F32)],
        [pltpu.VMEM((3 * cells, chans), BF16), pltpu.VMEM((pair, chans), BF16)], us=6, limit=20,
    )
    far, plus = lax.optimization_barrier((far, plus))
    far_other = swapped(far, core_link)
    side_conv, side_sum = call(
        functools.partial(side_kernel, plan), [spot], [side, side_other, even, odd, spread, turned], terms,
        [pltpu.VMEM((pair, chans), BF16)], us=2, limit=20,
    )
    outs = [shape((3, span, chans), BF16)]
    for begin, end in plan.cuts:
        outs += [shape(lead[1:] + (end - begin, part), BF16), shape(lead[1:] + (end - begin, part), F32)]
    down_dims = lead + (plan.down_rows, part)
    outs += [shape(down_dims, BF16), shape(down_dims, F32)]
    result = call(
        functools.partial(far_kernel, plan), [spot],
        [mine, side, far, far_other, even, odd, own_conv, own_sum, plus, side_conv, side_sum, spread, turned], outs,
        [pltpu.VMEM((pair, chans), BF16), pltpu.VMEM((3, wide, chans), F32), pltpu.VMEM(lead + (plan.rows, part), F32)],
        us=3, limit=20,
    )
    head = result[0]
    held = []
    for g in range(3):
        held += [result[2 + 2 * g], swapped(result[1 + 2 * g], plan.orders[g][0])]
    send, keep = call(
        functools.partial(single_kernel, plan, 0, 0), [spot], [result[8], swapped(result[7], core_link)],
        [shape(down_dims[1:], BF16), shape(down_dims[1:], F32)], limit=8,
    )
    down_held = [keep, swapped(send, plan.orders[0][0])]
    following = lax.ppermute(head, "tm", [(i + 1, i) for i in range(1, tm_count - 1, 2)])
    grads, ready = call(
        functools.partial(grads_kernel, plan), [spot],
        [mine, here_other, side, side_other, far, far_other, following, spread],
        [shape((3, (2 * half + 2) * ncols, chans), BF16), shape((8, part), F32)], us=1, limit=16,
    )
    middle, begun = call(
        functools.partial(middle_kernel, plan), [spot], [grads, weight],
        [shape((cells, chans), F32), shape((8, part), F32)], us=1, limit=16,
    )
    grad_input, done = call(
        functools.partial(input_kernel, plan), [spot], [flat, grads, middle, weight],
        [shape((cells, chans), BF16), shape((8, part), F32)], us=2, limit=24,
    )
    held = [held[:2] + down_held, held[2:4], held[4:6]]
    for step in (1, 2):
        for g in range(3):
            rows = plan.cuts[g][1] - plan.cuts[g][0] + (plan.down_rows if g == 0 else 0)
            dims = lead[step + 1 :] + (rows, part)
            send, keep = call(
                functools.partial(single_kernel, plan, g, step), [spot], held[g], [shape(dims, BF16), shape(dims, F32)],
                us=2.5, limit=8, after=[ready] if (g, step) == (2, 2) else (),
            )
            held[g] = [keep, swapped(send, plan.orders[g][step])]
    held = sum(held, [])
    for step in range(3, len(lead)):
        dims = lead[step + 1 :] + (plan.rows + plan.down_rows, part)
        send, keep = call(
            functools.partial(merge_kernel, plan, step), [spot], held, [shape(dims, BF16), shape(dims, F32)], limit=8,
            after=[begun] if step == 3 else (),
        )
        held = [keep, swapped(send, plan.orders[0][step])]
    arrived, done = lax.optimization_barrier((held[1], done))
    grad_conv, grad_down = call(
        functools.partial(join_kernel, plan), [spot], held + [swapped(held[0], core_link), swapped(arrived, core_link)],
        [shape((part // 2, 2 * plan.rows), F32), shape((part // 2, 2 * plan.down_rows), F32)],
        [pltpu.VMEM((part, 2 * plan.rows), F32), pltpu.VMEM((part, 2 * plan.down_rows), F32)],
        limit=8, after=[done],
    )
    return (grad_input.reshape(clip.shape), grad_conv.T, grad_down.T)


def solution(mesh):
    placed = (P("tm", "height", None, None), P(), P(), P("tm", "height", None, None))
    return jax.shard_map(
        body,
        mesh=mesh,
        in_specs=placed,
        out_specs=(P("tm", "height", None, None), P("height", "tm"), P("height", "tm")),
        check_vma=False,
    )
```
